32 devices in a mesh: seq: 4 (over z), dom: 8 (over y, x, core).
Axes of the slice: x: 2, y: 2, z: 4, core: 2. Of those that a mesh axis runs over, the one named last changes fastest.
Arguments:
- nodes: bfloat16 [8, 1536, 1024], P('dom', 'seq'), may hold values from -6 to 6
- norm_gain: float32 [1024], replicated, may hold values from 0.1 to 1.9
- input_proj: bfloat16 [1024, 3, 1024], replicated, may hold values from -0.1875 to 0.1875
- output_proj: bfloat16 [1024, 1024], replicated, may hold values from -0.1875 to 0.1875
- final_gain: float32 [1024], replicated, may hold values from 0.1 to 1.9
- block_list: int32 [96, 12], replicated, may hold values from -1 to 95, as said below
- block_count: int32 [96], replicated, may hold values from 8 to 12
Outputs:
- layer_out: bfloat16 [8, 1536, 1024], P('dom', 'seq')
The draws below stay inside these ranges and needn't reach their ends.
Inputs may be any that keep to these rules, and one draw needn't show every extreme that they name: `block_list`: entries 0 to block_count - 1 of a query block's list are live, the others are -1. Entry 0 is the query block itself, entries 1 to 3 are other blocks of its partition (1536 consecutive nodes), later live entries lie in other partitions, and no block appears twice in one list. Over all query blocks of one partition at most 2 distinct blocks of any one other partition are listed, and in every draw each partition lists exactly 2 blocks from some other partition.
All inputs are finite; a program needn't handle non-finite values.
Results may differ from the reference program's by a relative error of at most 0.014.
The reference program's roundings to bfloat16 on the way (of `normed`, `projected`, `weights` and `attended`) count: a program that leaves them out, or rounds other values in their place, can miss the bound.
Values may be sent and summed in bfloat16 or wider, within the bound.
A program may use at most 128 MiB of HBM per device.

```python
import jax
import jax.numpy as jnp
from jax import lax

D = 1024
H = 16
HD = 64
BLK = 128
KMAX = 12
CAP = 2
PARTS_SIZE = 8
PROWS = 1536
BP = 12
QBLOCKS = 96


def make_lists(key):
    base_key = jax.random.fold_in(key, 11)
    count_key, pick_key, perm_key, local_key = jax.random.split(base_key, 4)
    parts_index = jnp.arange(PARTS_SIZE)
    part_gap = (parts_index[None, :] - parts_index[:, None]) % PARTS_SIZE
    picked = jax.random.randint(pick_key, (PARTS_SIZE, PARTS_SIZE), 0, CAP + 1)
    picked = jnp.where((part_gap >= 1) & (part_gap <= 4), CAP, picked)
    picked = jnp.where(part_gap == 0, 0, picked)
    perm_keys = jax.random.split(perm_key, PARTS_SIZE * PARTS_SIZE)
    shuffled = jax.vmap(lambda subkey: jax.random.permutation(subkey, BP))(perm_keys).reshape(PARTS_SIZE, PARTS_SIZE, BP)
    chosen = jnp.arange(BP)[None, None, :] < picked[:, :, None]
    block_ids = parts_index[None, :, None] * BP + shuffled
    chosen = chosen.reshape(PARTS_SIZE, PARTS_SIZE * BP)
    block_ids = block_ids.reshape(PARTS_SIZE, PARTS_SIZE * BP)
    ordering = jnp.argsort(jnp.where(chosen, 0, 1), axis=1, stable=True)
    pool_ids = jnp.take_along_axis(block_ids, ordering, axis=1)
    pool_size = jnp.sum(chosen.astype(jnp.int32), axis=1)
    counts = jax.random.randint(count_key, (PARTS_SIZE, BP), KMAX - 4, KMAX + 1)
    local_keys = jax.random.split(local_key, PARTS_SIZE * BP)
    offsets = jax.vmap(lambda subkey: jax.random.permutation(subkey, BP - 1)[:3])(local_keys).reshape(PARTS_SIZE, BP, 3) + 1
    own_ids = parts_index[:, None] * BP + jnp.arange(BP)[None, :]
    near_ids = parts_index[:, None, None] * BP + (jnp.arange(BP)[None, :, None] + offsets) % BP
    far_slots = jnp.arange(KMAX - 4)
    far_live = far_slots[None, None, :] + 4 < counts[:, :, None]
    running = jnp.cumsum(far_live.reshape(PARTS_SIZE, -1).astype(jnp.int32), axis=1) - 1
    running = running % pool_size[:, None]
    far_ids = jnp.take_along_axis(pool_ids, running, axis=1).reshape(PARTS_SIZE, BP, KMAX - 4)
    listing = jnp.concatenate([own_ids[:, :, None], near_ids, far_ids], axis=2)
    live_slots = jnp.arange(KMAX)[None, None, :] < counts[:, :, None]
    listing = jnp.where(live_slots, listing, -1)
    return (listing.reshape(QBLOCKS, KMAX).astype(jnp.int32), counts.reshape(QBLOCKS).astype(jnp.int32))


def draw_block_list(key, part):
    return make_lists(key)[0]


def draw_block_count(key, part):
    return make_lists(key)[1]


def draw_nodes(key, part):
    rows_all = PARTS_SIZE * PROWS
    drawn_rows = jnp.clip(jax.random.normal(jax.random.fold_in(key, 3), (rows_all, D), jnp.float32), -6.0, 6.0)
    return drawn_rows.reshape(PARTS_SIZE, PROWS, D).astype(jnp.bfloat16)


def draw_input_proj(key, part):
    scale_factor = D ** (-0.5)
    weights_drawn = jnp.clip(jax.random.normal(jax.random.fold_in(key, 7), (D, 3, D), jnp.float32), -6.0, 6.0) * scale_factor
    return weights_drawn.astype(jnp.bfloat16)


def noise(rng, extent, width, bound, dtype=jnp.bfloat16):
    result = jax.random.normal(rng, extent, jnp.float32) * width
    return jnp.minimum(jnp.maximum(result, -bound), bound).astype(dtype)


def setup_inputs(seed: int = 0) -> dict:
    seeds = jax.random.split(jax.random.key(seed), 8)
    nodes = draw_nodes(jax.random.fold_in(seeds[7], 71), 0)
    norm_gain = jnp.clip(1.0 + 0.18 * jax.random.normal(seeds[1], (D,), jnp.float32), 0.1, 1.9)
    input_proj = draw_input_proj(jax.random.fold_in(seeds[7], 71), 0)
    output_proj = noise(seeds[3], (D, D), D ** -0.5, 0.1875)
    final_gain = jnp.clip(1.0 + 0.18 * jax.random.normal(seeds[4], (D,), jnp.float32), 0.1, 1.9)
    block_list = draw_block_list(jax.random.fold_in(seeds[7], 71), 0)
    block_count = draw_block_count(jax.random.fold_in(seeds[7], 71), 0)
    return {"nodes": nodes, "norm_gain": norm_gain, "input_proj": input_proj, "output_proj": output_proj, "final_gain": final_gain, "block_list": block_list, "block_count": block_count}


def layer_norm(inputs_row, gain_vector):
    widened = inputs_row.astype(jnp.float32)
    center = lax.optimization_barrier(jnp.mean(widened, axis=-1, keepdims=True))
    spread = lax.optimization_barrier(jnp.mean(jnp.square(widened - center), axis=-1, keepdims=True))
    return ((widened - center) * lax.rsqrt(spread + 1e-05) * gain_vector.astype(jnp.float32)).astype(jnp.bfloat16)

def rms_scale(inputs_row, gain_vector):
    spread = lax.optimization_barrier(jnp.mean(jnp.square(inputs_row), axis=-1, keepdims=True))
    return (inputs_row * lax.rsqrt(spread + 1e-05) * gain_vector.astype(jnp.float32)).astype(jnp.bfloat16)

def reference(nodes, norm_gain, input_proj, output_proj, final_gain, block_list, block_count):
    flat_nodes = nodes.reshape(PARTS_SIZE * PROWS, D)
    normed = layer_norm(flat_nodes, norm_gain)
    projected = jnp.dot(normed, input_proj.reshape(D, 3 * D), preferred_element_type=jnp.float32).astype(jnp.bfloat16)
    projected = lax.optimization_barrier(projected)
    projected = projected.reshape(QBLOCKS, BLK, 3, H, HD)
    queries = projected[:, :, 0]
    key_rows = projected[:, :, 1]
    value_rows = projected[:, :, 2]
    live_slots = jnp.arange(KMAX)[None, :] < block_count[:, None]
    safe_list = jnp.where(live_slots, block_list, 0).astype(jnp.int32)
    groups = QBLOCKS // 4

    def attend(inputs):
        query_group, index_group, live_group = inputs
        key_group = key_rows[index_group].astype(jnp.float32)
        value_group = value_rows[index_group].astype(jnp.float32)
        scores = jnp.einsum('qrhd,qjkhd->qhrjk', query_group.astype(jnp.float32), key_group) * HD ** (-0.5)
        scores = jnp.where(live_group[:, None, None, :, None], scores, -jnp.inf)
        score_peak = lax.optimization_barrier(jnp.max(scores, axis=(3, 4), keepdims=True))
        weights = jnp.exp(scores - score_peak)
        weight_total = lax.optimization_barrier(jnp.sum(weights, axis=(3, 4), keepdims=True))
        weights = (weights / weight_total).astype(jnp.bfloat16)
        weights = lax.optimization_barrier(weights).astype(jnp.float32)
        head_mix = jnp.einsum('qhrjk,qjkhd->qrhd', weights, value_group)
        return head_mix.astype(jnp.bfloat16)
    attended = lax.map(attend, (queries.reshape(groups, 4, BLK, H, HD), safe_list.reshape(groups, 4, KMAX), live_slots.reshape(groups, 4, KMAX)))
    attended = attended.reshape(PARTS_SIZE * PROWS, D)
    mapped = jnp.dot(attended, output_proj, preferred_element_type=jnp.float32)
    return rms_scale(mapped, final_gain).reshape(PARTS_SIZE, PROWS, D)
```

```python
import functools
import math

import jax
import jax.numpy as jnp
from jax import lax
from jax.experimental import pallas as pl
from jax.experimental.pallas import tpu as pltpu
from jax.sharding import PartitionSpec as P

HD = 64
BLK = 128
KMAX = 12
CAP = 2
NEAR = 4
GW = 256
GH = GW // HD
CHUNKS = 4
MESH = pl.DeviceIdType.MESH


def dot(a, b, dims=((1,), (0,))):
    return lax.dot_general(a, b, (dims, ((), ())), preferred_element_type=jnp.float32)


def gather_kernel(seq_size, dom_size, pick_ref, nodes_ref, gain_ref, *refs):
    local = refs[:CHUNKS]
    remote = refs[CHUNKS]
    stage, zsend, zrecv, dsend, drecv = refs[CHUNKS + 1 :]
    rows, width = nodes_ref.shape
    cw = width // CHUNKS
    z = lax.axis_index("seq")
    me = lax.axis_index("dom")
    last = seq_size - 1

    barrier = pltpu.get_barrier_semaphore()

    @pl.when(z > 0)
    def _():
        pl.semaphore_signal(barrier, inc=1, device_id=(z - 1, me), device_id_type=MESH)

    @pl.when(z < last)
    def _():
        pl.semaphore_signal(barrier, inc=1, device_id=(z + 1, me), device_id_type=MESH)

    for o in range(1, dom_size):
        pl.semaphore_signal(
            barrier, inc=1, device_id=(z, lax.rem(me + o, dom_size)), device_id_type=MESH
        )

    step = BLK
    held = rows // BLK
    for r in range(0, rows, step):
        wide = nodes_ref[r : r + step, :].astype(jnp.float32)
        center = jnp.mean(wide, axis=-1, keepdims=True)
        moved = wide - center
        spread = jnp.mean(jnp.square(moved), axis=-1, keepdims=True)
        normed = (moved * lax.rsqrt(spread + 1e-05) * gain_ref[...]).astype(jnp.bfloat16)
        for c in range(CHUNKS):
            local[c][z * held + r // step] = normed[:, c * cw : (c + 1) * cw]

    @pl.when((z > 0) & (z < last))
    def _():
        pl.semaphore_wait(barrier, dom_size + 1)

    @pl.when((z == 0) | (z == last))
    def _():
        pl.semaphore_wait(barrier, dom_size)

    def along(c, d, t):
        source = z - (t - 1) if d == 0 else z + (t - 1)
        target = z + 1 if d == 0 else z - 1
        block = local[c].at[pl.ds(source * held, held)]
        return pltpu.make_async_remote_copy(
            src_ref=block,
            dst_ref=block,
            send_sem=zsend.at[d, t - 1, c],
            recv_sem=zrecv.at[d, t - 1, c],
            device_id=(target, me),
            device_id_type=MESH,
        )

    def arriving(c, d, t):
        source = z - t if d == 0 else z + t
        block = local[c].at[pl.ds(source * held, held)]
        return pltpu.make_async_remote_copy(
            src_ref=block,
            dst_ref=block,
            send_sem=zsend.at[d, t - 1, c],
            recv_sem=zrecv.at[d, t - 1, c],
            device_id=(z - 1 if d == 0 else z + 1, me),
            device_id_type=MESH,
        )

    def sends(d, t):
        return (z >= t - 1) & (z < last) if d == 0 else (z <= last - (t - 1)) & (z > 0)

    def gets(d, t):
        return z >= t if d == 0 else z <= last - t

    def begin(c):
        for d in range(2):

            @pl.when(sends(d, 1))
            def _():
                along(c, d, 1).start()

    def across(c, o):
        target = lax.rem(me + o, dom_size)
        return pltpu.make_async_remote_copy(
            src_ref=stage.at[c, o - 1],
            dst_ref=remote.at[c, pl.ds(me * CAP, CAP)],
            send_sem=dsend.at[c, o - 1],
            recv_sem=drecv.at[c, o - 1],
            device_id=(z, target),
            device_id_type=MESH,
        )

    begin(0)
    if CHUNKS > 1:
        begin(1)
    for c in range(CHUNKS):
        for k in range(CAP):
            remote[c, me * CAP + k] = jnp.zeros((BLK, cw), jnp.bfloat16)
    for c in range(CHUNKS):
        for t in range(1, seq_size):
            for d in range(2):

                @pl.when(gets(d, t))
                def _():
                    arriving(c, d, t).wait_recv()

                if t < last:

                    @pl.when(sends(d, t + 1))
                    def _():
                        along(c, d, t + 1).start()

        if c + 2 < CHUNKS:
            begin(c + 2)
        for o in range(1, dom_size):
            target = lax.rem(me + o, dom_size)
            for k in range(CAP):
                block = pick_ref[target * CAP + k]
                stage[c, o - 1, k] = local[c][block]
            across(c, o).start()
    for c in range(CHUNKS):
        for o in range(1, dom_size):
            source = lax.rem(me + dom_size - o, dom_size)
            pltpu.make_async_remote_copy(
                src_ref=stage.at[c, o - 1],
                dst_ref=remote.at[c, pl.ds(source * CAP, CAP)],
                send_sem=dsend.at[c, o - 1],
                recv_sem=drecv.at[c, o - 1],
                device_id=(z, source),
                device_id_type=MESH,
            ).wait_recv()
            across(c, o).wait_send()
        for t in range(1, seq_size):
            for d in range(2):

                @pl.when(sends(d, t))
                def _():
                    along(c, d, t).wait_send()


def gather_rows(seq_size, dom_size, picks, node_rows, norm_gain):
    rows, width = node_rows.shape
    cw = width // CHUNKS
    vmem = pl.BlockSpec(memory_space=pltpu.VMEM)
    out = [jax.ShapeDtypeStruct((rows * seq_size // BLK, BLK, cw), jnp.bfloat16)] * CHUNKS
    out.append(jax.ShapeDtypeStruct((CHUNKS, dom_size * CAP, BLK, cw), jnp.bfloat16))
    return pl.pallas_call(
        functools.partial(gather_kernel, seq_size, dom_size),
        out_shape=out,
        in_specs=[pl.BlockSpec(memory_space=pltpu.SMEM), vmem, vmem],
        out_specs=[vmem] * (CHUNKS + 1),
        scratch_shapes=[
            pltpu.VMEM((CHUNKS, dom_size - 1, CAP, BLK, cw), jnp.bfloat16),
            pltpu.SemaphoreType.DMA((2, seq_size - 1, CHUNKS)),
            pltpu.SemaphoreType.DMA((2, seq_size - 1, CHUNKS)),
            pltpu.SemaphoreType.DMA((CHUNKS, dom_size - 1)),
            pltpu.SemaphoreType.DMA((CHUNKS, dom_size - 1)),
        ],
        compiler_params=pltpu.CompilerParams(
            collective_id=0, has_side_effects=True, vmem_limit_bytes=56 * 2**20
        ),
        name="gather_rows",
    )(picks, node_rows, norm_gain)


def attend_kernel(table_ref, meta_ref, *refs):
    local = refs[:CHUNKS]
    remote, w_ref, wo_ref, gain_ref, out_ref, k_ref, vt_ref, s_ref, mapped_ref = refs[CHUNKS:]
    g = pl.program_id(0)
    rows = out_ref.shape[0]
    local_blocks = local[0].shape[0]
    remote_blocks = remote.shape[1]
    wk = w_ref[1]
    wvt = w_ref[2].T

    def keep(x, base):
        n = x.shape[0]
        k_ref[pl.ds(pl.multiple_of(base * BLK, BLK), n), :] = dot(x, wk).astype(jnp.bfloat16)
        vt = dot(wvt, x, ((1,), (1,))).astype(jnp.bfloat16)
        for i in range(n // BLK):
            vt_ref[base + i] = vt[:, i * BLK : (i + 1) * BLK]

    def project(refs, base, count):
        step = max(n for n in range(1, 9) if count % n == 0)

        @pl.loop(0, count // step)
        def _(i):
            at = pl.ds(i * step, step)
            x = jnp.concatenate([c[at].reshape(step * BLK, -1) for c in refs], axis=1)
            keep(x, base + i * step)

    project(local, 0, local_blocks)
    project([remote.at[c] for c in range(CHUNKS)], local_blocks, remote_blocks)

    mine = pl.ds(meta_ref[0], rows // BLK)
    queries = dot(jnp.concatenate([c[mine].reshape(rows, -1) for c in local], axis=1), w_ref[0])
    queries = queries.astype(jnp.bfloat16) * jnp.bfloat16(HD**-0.5)

    head_of = lax.broadcasted_iota(jnp.int32, (GW, BLK), 0) // HD
    def score(b):
        qt = queries[b * BLK : (b + 1) * BLK, :].astype(jnp.float32).T
        spread = jnp.concatenate(
            [jnp.where(head_of == h, qt, 0.0) for h in range(GH)], axis=1
        ).astype(jnp.bfloat16)
        peak = None
        for j in range(KMAX):
            entry = table_ref[b * KMAX + j]
            keys = k_ref[pl.ds(pl.multiple_of(entry * BLK, BLK), BLK), :]
            scores = dot(keys, spread)
            if j >= KMAX - 4:
                scores = jnp.where(j < meta_ref[1 + b], scores, -jnp.inf)
            s_ref[b % 2, j] = scores
            top = jnp.max(scores.reshape(BLK // 8, 8, GH * BLK), axis=0)
            peak = top if peak is None else jnp.maximum(peak, top)
        return jnp.max(peak, axis=0, keepdims=True)

    def blend(b, peak):
        total = jnp.zeros((8, GH * BLK), jnp.float32)
        mix = jnp.zeros((GW, GH * BLK), jnp.float32)
        for j in range(0, KMAX, 2):
            parts = [jnp.exp(s_ref[b % 2, j + i] - peak) for i in range(2)]
            total += jnp.sum((parts[0] + parts[1]).reshape(BLK // 8, 8, GH * BLK), axis=0)
            weights = jnp.concatenate([p.astype(jnp.bfloat16) for p in parts], axis=0)
            values = jnp.concatenate([vt_ref[table_ref[b * KMAX + j + i]] for i in range(2)], axis=1)
            mix += dot(values, weights)
        scale = 1.0 / jnp.sum(total, axis=0, keepdims=True)
        attended = jnp.concatenate(
            [
                mix[h * HD : (h + 1) * HD, h * BLK : (h + 1) * BLK] * scale[:, h * BLK : (h + 1) * BLK]
                for h in range(GH)
            ],
            axis=0,
        )
        term = dot(attended.T.astype(jnp.bfloat16), wo_ref[...])
        at = slice(b * BLK, (b + 1) * BLK)
        mapped_ref[at, :] = jnp.where(g == 0, 0.0, mapped_ref[at, :]) + term

    query_blocks = rows // BLK
    peak = score(0)
    for b in range(query_blocks):
        later = score(b + 1) if b + 1 < query_blocks else None
        blend(b, peak)
        peak = later

    @pl.when(g == pl.num_programs(0) - 1)
    def _():
        mapped = mapped_ref[...]
        spread = jnp.mean(jnp.square(mapped), axis=-1, keepdims=True)
        out_ref[...] = (mapped * lax.rsqrt(spread + 1e-05) * gain_ref[...]).astype(jnp.bfloat16)


def attend_rows(table, meta, local, remote, weights, output_proj, final_gain, rows):
    width = output_proj.shape[0]
    blocks = local[0].shape[0] + remote.shape[1]
    vmem = pl.BlockSpec(memory_space=pltpu.VMEM)
    return pl.pallas_call(
        attend_kernel,
        out_shape=jax.ShapeDtypeStruct((rows, width), jnp.bfloat16),
        grid_spec=pltpu.PrefetchScalarGridSpec(
            num_scalar_prefetch=2,
            grid=(width // GW,),
            in_specs=[vmem] * (CHUNKS + 1)
            + [
                pl.BlockSpec((3, width, GW), lambda g, *_: (0, 0, g)),
                pl.BlockSpec((GW, width), lambda g, *_: (g, 0)),
                vmem,
            ],
            out_specs=pl.BlockSpec((rows, width), lambda g, *_: (0, 0)),
            scratch_shapes=[
                pltpu.VMEM((blocks * BLK, GW), jnp.bfloat16),
                pltpu.VMEM((blocks, GW, BLK), jnp.bfloat16),
                pltpu.VMEM((2, KMAX, BLK, GH * BLK), jnp.float32),
                pltpu.VMEM((rows, width), jnp.float32),
            ],
        ),
        compiler_params=pltpu.CompilerParams(vmem_limit_bytes=60 * 2**20),
        name="attend_rows",
    )(table, meta, *local, remote, weights, output_proj, final_gain)


def plan_lists(block_list, block_count, blocks_here, query_blocks):
    dom_size = lax.axis_size("dom")
    me = lax.axis_index("dom")
    z = lax.axis_index("seq")
    live = jnp.arange(KMAX)[None, :] < block_count[:, None]
    listed = jnp.where(live, block_list, -1).reshape(dom_size, blocks_here * KMAX)
    mine = me * blocks_here + jnp.arange(blocks_here)
    asked = jnp.any(listed[:, :, None] == mine[None, None, :], axis=1)
    before = jnp.arange(blocks_here)[:, None] < jnp.arange(blocks_here)[None, :]
    rank = jnp.sum(asked[:, :, None] & before[None], axis=1, dtype=jnp.int32)
    hit = asked[:, None, :] & (rank[:, None, :] == jnp.arange(CAP)[None, :, None])
    picks = jnp.sum(jnp.where(hit, jnp.arange(blocks_here)[None, None, :], 0), axis=2)
    every = jnp.arange(dom_size * blocks_here)
    ours = lax.dynamic_slice_in_dim(listed, me, 1, 0).reshape(-1)
    wanted = jnp.any(ours[:, None] == every[None, :], axis=0)
    entries = lax.dynamic_slice_in_dim(ours, z * query_blocks * KMAX, query_blocks * KMAX)
    safe = jnp.where(entries >= 0, entries, me * blocks_here)
    source = safe // blocks_here
    lower = (every[None, :] < safe[:, None]) & (every[None, :] >= (source * blocks_here)[:, None])
    slot = jnp.sum(lower & wanted[None, :], axis=1, dtype=jnp.int32)
    table = jnp.where(source == me, safe - me * blocks_here, blocks_here + source * CAP + slot)
    counts = lax.dynamic_slice_in_dim(block_count, me * blocks_here + z * query_blocks, query_blocks)
    meta = jnp.concatenate([jnp.reshape(z * query_blocks, (1,)), counts])
    return picks.reshape(-1), table.astype(jnp.int32), meta.astype(jnp.int32)


AHEAD = 2
UNIT = 16
SPLIT = 64
FAR = 2**30


def fused_kernel(
    seq_size, dom_size, lists_ref, entries_ref, counts_ref, nodes_ref, gain_ref, final_ref, w_hbm, wo_hbm,
    out_ref, x_ref, snap_ref, stage_ref, w_ref, kv_ref, q_ref, s_ref, peak_ref, sum_ref, near_ref,
    att_ref, pick_ref, first_ref, table_ref, zsend, zrecv, dsend, drecv, wsem,
):
    rows, width = nodes_ref.shape
    held = rows // BLK
    local_blocks = held * seq_size
    far_blocks = dom_size * CAP
    units = BLK // UNIT
    groups = width // GW
    heads = GH * BLK
    z = lax.axis_index("seq")
    me = lax.axis_index("dom")
    last = seq_size - 1

    barrier = pltpu.get_barrier_semaphore()

    @pl.when(z > 0)
    def _():
        pl.semaphore_signal(barrier, inc=1, device_id=(z - 1, me), device_id_type=MESH)

    @pl.when(z < last)
    def _():
        pl.semaphore_signal(barrier, inc=1, device_id=(z + 1, me), device_id_type=MESH)

    for o in range(1, dom_size):
        pl.semaphore_signal(
            barrier, inc=1, device_id=(z, lax.rem(me + o, dom_size)), device_id_type=MESH
        )

    loads = [pltpu.make_async_copy(w_hbm.at[i], w_ref.at[i], wsem.at[i]) for i in range(3)]
    load_out = pltpu.make_async_copy(wo_hbm, w_ref.at[0], wsem.at[3])
    for load in loads:
        load.start()

    for r in range(held):
        wide = nodes_ref[r * BLK : (r + 1) * BLK, :].astype(jnp.float32)
        center = jnp.mean(wide, axis=-1, keepdims=True)
        moved = wide - center
        spread = jnp.mean(jnp.square(moved), axis=-1, keepdims=True)
        normed = (moved * lax.rsqrt(spread + 1e-05) * gain_ref[...]).astype(jnp.bfloat16)
        for u in range(units):
            x_ref[u, z * held + r] = normed[u * UNIT : (u + 1) * UNIT, :]

    @pl.when((z > 0) & (z < last))
    def _():
        pl.semaphore_wait(barrier, dom_size + 1)

    @pl.when((z == 0) | (z == last))
    def _():
        pl.semaphore_wait(barrier, dom_size)

    def hop(u, d, t, source, target):
        block = x_ref.at[u, pl.ds(source * held, held)]
        return pltpu.make_async_remote_copy(
            src_ref=block,
            dst_ref=block,
            send_sem=zsend.at[d, t - 1, u],
            recv_sem=zrecv.at[d, t - 1, u],
            device_id=(target, me),
            device_id_type=MESH,
        )

    def along(u, d, t):
        return hop(u, d, t, z - (t - 1) if d == 0 else z + (t - 1), z + 1 if d == 0 else z - 1)

    def arriving(u, d, t):
        return hop(u, d, t, z - t if d == 0 else z + t, z - 1 if d == 0 else z + 1)

    def sends(d, t):
        return (z >= t - 1) & (z < last) if d == 0 else (z <= last - (t - 1)) & (z > 0)

    def gets(d, t):
        return z >= t if d == 0 else z <= last - t

    def begin(u, inner):
        for d in range(2):
            edge = 0 if d == 0 else last

            @pl.when(sends(d, 1) & ((z != edge) if inner else (z == edge)))
            def _():
                along(u, d, 1).start()

    def picked(u, o, source, partner):
        return pltpu.make_async_remote_copy(
            src_ref=stage_ref.at[u, o - 1],
            dst_ref=x_ref.at[u, pl.ds(local_blocks + source * CAP, CAP)],
            send_sem=dsend.at[u, o - 1],
            recv_sem=drecv.at[u, o - 1],
            device_id=(z, partner),
            device_id_type=MESH,
        )

    def across(u, o):
        return picked(u, o, me, lax.rem(me + o, dom_size))

    def take(u):
        for o in range(1, dom_size):
            source = lax.rem(me + dom_size - o, dom_size)
            picked(u, o, source, source).wait_recv()

    for u in range(units):
        begin(u, False)
        if u < AHEAD:
            begin(u, True)

    lists = lists_ref[...]
    lane = lax.broadcasted_iota(jnp.int32, lists.shape, 1)
    mine = (lists >= me * local_blocks) & (lists < (me + 1) * local_blocks)
    for o in range(1, dom_size):
        target = lax.rem(me + o, dom_size)
        theirs = (lane >= target * local_blocks) & (lane < (target + 1) * local_blocks)
        low = jnp.min(jnp.where(mine & theirs, lists, FAR))
        high = jnp.max(jnp.where(mine & theirs, lists, -1))
        pick_ref[(o - 1) * CAP] = jnp.where(low < FAR, low - me * local_blocks, 0)
        pick_ref[(o - 1) * CAP + 1] = jnp.where(high >= 0, high - me * local_blocks, 0)
    ours = (lane >= me * local_blocks) & (lane < (me + 1) * local_blocks)
    for s in range(dom_size):
        inside = (lists >= s * local_blocks) & (lists < (s + 1) * local_blocks)
        first_ref[s] = jnp.min(jnp.where(ours & inside, lists, FAR))
    at = me * local_blocks + z * held
    for b in range(held):
        for j in range(KMAX):
            entry = entries_ref[j, at + b]
            slot = z * held + b
            if j < NEAR:
                inside = (entry >= me * local_blocks) & (entry < (me + 1) * local_blocks)
                table_ref[b * KMAX + j] = jnp.where(inside, entry - me * local_blocks, slot)
            else:
                for s in range(dom_size):
                    place = local_blocks + s * CAP + jnp.where(entry == first_ref[s], 0, 1)
                    inside = (entry >= s * local_blocks) & (entry < (s + 1) * local_blocks)
                    slot = jnp.where(inside, place, slot)
                table_ref[b * KMAX + j] = slot

    for u in range(units):
        for k in range(CAP):
            x_ref[u, local_blocks + me * CAP + k] = jnp.zeros((UNIT, width), jnp.bfloat16)

    def project(kv, first, count, u, n):
        blocks = slice(first, first + count)
        x = x_ref[pl.ds(u, n), blocks].reshape(n * count * UNIT, width)
        for g in range(groups):
            cols = slice(g * GW, (g + 1) * GW)
            made = dot(x, w_ref[1 + kv, :, cols]).astype(jnp.bfloat16).reshape(n, count, UNIT, GW)
            for i in range(n):
                at_rows = pl.ds(pl.multiple_of((u + i) * UNIT, UNIT), UNIT)
                kv_ref[kv, blocks, at_rows, cols] = made[i]

    def project_queries():
        for load in loads:
            load.wait()
        x = x_ref[:, pl.ds(z * held, held)].reshape(rows, width)
        for g in range(groups):
            cols = slice(g * GW, (g + 1) * GW)
            made = dot(x, w_ref[0, :, cols]).astype(jnp.bfloat16) * jnp.bfloat16(HD**-0.5)
            q_ref[:, :, :, cols] = made.reshape(units, held, UNIT, GW)
        load_out.start()

    head_of = lax.broadcasted_iota(jnp.int32, (BLK, GW), 1) // HD

    def attend(b, start, end):
        span = end - start
        tiles = KMAX * span // BLK
        each = BLK // span
        nth = lax.broadcasted_iota(jnp.int32, (1, BLK), 1) // span

        def gathered(kv, g, tile, n):
            entries = range(tile * each, (tile + n) * each)
            return jnp.concatenate(
                [kv_ref[kv, table_ref[b * KMAX + j], start:end, g * GW : (g + 1) * GW] for j in entries],
                axis=0,
            )

        def spans():
            return [(i, min(2, tiles - i)) for i in range(0, tiles, 2)]

        def score(g):
            q = q_ref[:, b, :, g * GW : (g + 1) * GW].reshape(BLK, GW)
            wide = jnp.concatenate([jnp.where(head_of == h, q, jnp.bfloat16(0)) for h in range(GH)], axis=0)
            peak = None
            for tile, n in spans():
                both = dot(wide, gathered(0, g, tile, n), ((1,), (1,)))
                for i in range(n):
                    scores = both[:, i * BLK : (i + 1) * BLK]
                    if (tile + i + 1) * each > KMAX - 4:
                        live = nth + (tile + i) * each < counts_ref[at + b]
                        scores = jnp.where(live, scores, -jnp.inf)
                    s_ref[(g % 2) * MOST + tile + i] = scores
                    peak = scores if peak is None else jnp.maximum(peak, scores)
            peak = jnp.broadcast_to(jnp.max(peak, axis=1, keepdims=True), (heads, BLK))
            return peak if start == 0 else jnp.maximum(peak, peak_ref[b * groups + g])

        def blend(g, peak):
            total = jnp.zeros((heads, BLK), jnp.float32)
            mix = jnp.zeros((heads, GW), jnp.float32)
            for tile, n in spans():
                parts = [jnp.exp(s_ref[(g % 2) * MOST + tile + i] - peak) for i in range(n)]
                for part in parts:
                    total += part
                weights = jnp.concatenate([part.astype(jnp.bfloat16) for part in parts], axis=1)
                mix += dot(weights, gathered(1, g, tile, n))
            return jnp.broadcast_to(jnp.sum(total, axis=1, keepdims=True), (heads, BLK)), mix

        def own_heads(part_of):
            kept = None
            for h in range(GH):
                part = jnp.where(head_of == h, part_of(h), 0.0)
                kept = part if kept is None else kept + part
            return kept

        def rows_of(x, h):
            return x[h * BLK : (h + 1) * BLK]

        def over(x, h):
            return jnp.concatenate([rows_of(x, h)] * (GW // BLK), axis=1)

        peak = score(0)
        for g in range(groups):
            n = b * groups + g
            later = score(g + 1) if g + 1 < groups else None
            total, mix = blend(g, peak)
            if start == 0:
                kept = own_heads(lambda h: rows_of(mix, h))
            else:
                fade = jnp.exp(peak_ref[n] - peak)
                total = total + sum_ref[n] * fade
                near = near_ref[n]
                if end == BLK:
                    scale = 1.0 / total
                    fade = fade * scale
                    kept = own_heads(lambda h: rows_of(mix, h) * over(scale, h) + near * over(fade, h))
                else:
                    kept = own_heads(lambda h: rows_of(mix, h) + near * over(fade, h))
            if end == BLK:
                at_rows = pl.ds(pl.multiple_of(b * BLK, BLK), BLK)
                att_ref[at_rows, g * GW : (g + 1) * GW] = kept.astype(jnp.bfloat16)
            else:
                peak_ref[n] = peak
                sum_ref[n] = total
                near_ref[n] = kept
            peak = later

    @pl.loop(0, units)
    def _(u):
        odd = lax.rem(u, 2)
        for t in range(1, seq_size):
            for d in range(2):

                @pl.when(gets(d, t))
                def _():
                    arriving(u, d, t).wait_recv()

                if t < last:

                    @pl.when(sends(d, t + 1))
                    def _():
                        along(u, d, t + 1).start()

            if t == last:

                @pl.when(u + AHEAD < units)
                def _():
                    begin(u + AHEAD, True)

                snap_ref[...] = x_ref[u, 0:local_blocks]
                for o in range(1, dom_size):
                    for k in range(CAP):
                        stage_ref[u, o - 1, k] = snap_ref[pick_ref[(o - 1) * CAP + k]]
                    across(u, o).start()

                @pl.when(u == 0)
                def _():
                    project_queries()

            for kv in range(2):
                if t == min(kv + 1, last):

                    @pl.when((u >= 2) & (odd == 0))
                    def _():
                        project(kv, 0, local_blocks, u - 2, 2)

                    @pl.when((u >= 3) & (odd == 1))
                    def _():
                        if kv == 0:
                            take(u - 3)
                            take(u - 2)
                        project(kv, local_blocks, far_blocks, u - 3, 2)

            if t == last:

                @pl.when(u >= units - 2)
                def _():
                    late = u - (units - 2)
                    most = held - held // 2

                    @pl.loop(late * most, most + late * (held - most))
                    def _(b):
                        attend(b, 0, SPLIT)

    for kv in range(2):
        project(kv, 0, local_blocks, units - 2, 2)

    @pl.loop(units - 2, units)
    def _(u):
        take(u)
        for kv in range(2):
            project(kv, local_blocks, far_blocks, u, 1)

    @pl.loop(0, held)
    def _(b):
        attend(b, SPLIT, BLK)

    load_out.wait()
    part = GW // BLK
    squares = jnp.zeros((rows, BLK), jnp.float32)
    for g in range(groups):
        mapped = dot(att_ref[...], w_ref[0, :, g * GW : (g + 1) * GW])
        for i in range(part):
            piece_of = mapped[:, i * BLK : (i + 1) * BLK]
            s_ref[g * part + i, 0:rows, :] = piece_of
            squares += jnp.square(piece_of)
    norm = lax.rsqrt(jnp.sum(squares, axis=1, keepdims=True) * (1.0 / width) + 1e-05)
    for i in range(groups * part):
        cols = slice(i * BLK, (i + 1) * BLK)
        out_ref[:, cols] = (s_ref[i, 0:rows, :] * norm * final_ref[:, cols]).astype(jnp.bfloat16)

    @pl.loop(0, units)
    def _(u):
        for o in range(1, dom_size):
            across(u, o).wait_send()
        for t in range(1, seq_size):
            for d in range(2):

                @pl.when(sends(d, t))
                def _():
                    along(u, d, t).wait_send()


MOST = KMAX * max(SPLIT, BLK - SPLIT) // BLK


def fused_scratch(seq_size, dom_size, rows, width):
    units = BLK // UNIT
    held = rows // BLK
    local_blocks = held * seq_size
    blocks = local_blocks + dom_size * CAP
    steps = held * (width // GW)
    heads = GH * BLK
    f32, bf16, i32 = jnp.float32, jnp.bfloat16, jnp.int32
    arrays = [
        ((units, blocks, UNIT, width), bf16),
        ((local_blocks, UNIT, width), bf16),
        ((units, dom_size - 1, CAP, UNIT, width), bf16),
        ((3, width, width), bf16),
        ((2, blocks, BLK, width), bf16),
        ((units, held, UNIT, width), bf16),
        ((2 * MOST, heads, BLK), f32),
        ((steps, heads, BLK), f32),
        ((steps, heads, BLK), f32),
        ((steps, BLK, GW), f32),
        ((rows, width), bf16),
    ]
    size = sum(math.prod(shape) * jnp.dtype(kind).itemsize for shape, kind in arrays)
    scratch = [pltpu.VMEM(shape, kind) for shape, kind in arrays]
    scratch += [pltpu.SMEM((n,), i32) for n in (CAP * (dom_size - 1), dom_size, held * KMAX)]
    scratch += [
        pltpu.SemaphoreType.DMA((2, seq_size - 1, units)),
        pltpu.SemaphoreType.DMA((2, seq_size - 1, units)),
        pltpu.SemaphoreType.DMA((units, dom_size - 1)),
        pltpu.SemaphoreType.DMA((units, dom_size - 1)),
        pltpu.SemaphoreType.DMA((4,)),
    ]
    return scratch, width <= BLK * 2 * MOST and rows <= heads and size < 50 * 2**20


def fused_layer(seq_size, dom_size, scratch, node_rows, norm_gain, weights, output_proj, final_gain, lists, counts):
    vmem = pl.BlockSpec(memory_space=pltpu.VMEM)
    smem = pl.BlockSpec(memory_space=pltpu.SMEM)
    hbm = pl.BlockSpec(memory_space=pl.ANY)
    return pl.pallas_call(
        functools.partial(fused_kernel, seq_size, dom_size),
        out_shape=jax.ShapeDtypeStruct(node_rows.shape, jnp.bfloat16),
        in_specs=[vmem, smem, smem, vmem, vmem, vmem, hbm, hbm],
        out_specs=vmem,
        scratch_shapes=scratch,
        compiler_params=pltpu.CompilerParams(
            collective_id=1, has_side_effects=True, vmem_limit_bytes=60 * 2**20
        ),
        name="fused_layer",
    )(lists, lists, counts, node_rows, norm_gain, final_gain, weights, output_proj)


def on_device(nodes, norm_gain, input_proj, output_proj, final_gain, block_list, block_count):
    node_rows = nodes[0]
    rows = node_rows.shape[0]
    seq_size = lax.axis_size("seq")
    dom_size = lax.axis_size("dom")
    weights = jnp.transpose(input_proj, (1, 0, 2))
    scratch, fits = fused_scratch(seq_size, dom_size, rows, node_rows.shape[1])
    if fits:
        out = fused_layer(
            seq_size, dom_size, scratch, node_rows, norm_gain[None, :], weights, output_proj,
            final_gain[None, :], block_list.T, block_count,
        )
        return out[None]
    blocks_here = rows * seq_size // BLK
    picks, table, meta = plan_lists(block_list, block_count, blocks_here, rows // BLK)
    *local, remote = gather_rows(seq_size, dom_size, picks, node_rows, norm_gain[None, :])
    out = attend_rows(
        table, meta, local, remote, weights, output_proj, final_gain[None, :], rows,
    )
    return out[None]


def solution(mesh):
    placed = (P("dom", "seq", None), P(), P(), P(), P(), P(), P())
    return jax.shard_map(
        on_device, mesh=mesh, in_specs=placed, out_specs=P("dom", "seq", None), check_vma=False
    )
```

```python
import functools
import math

import jax
import jax.numpy as jnp
from jax import lax
from jax.experimental import pallas as pl
from jax.experimental.pallas import tpu as pltpu
from jax.sharding import PartitionSpec as P

HD = 64
BLK = 128
KMAX = 12
CAP = 2
NEAR = 4
GW = 256
GH = GW // HD
CHUNKS = 4
MESH = pl.DeviceIdType.MESH


def dot(a, b, dims=((1,), (0,))):
    return lax.dot_general(a, b, (dims, ((), ())), preferred_element_type=jnp.float32)


def gather_kernel(seq_size, dom_size, pick_ref, nodes_ref, gain_ref, *refs):
    local = refs[:CHUNKS]
    remote = refs[CHUNKS]
    stage, zsend, zrecv, dsend, drecv = refs[CHUNKS + 1 :]
    rows, width = nodes_ref.shape
    cw = width // CHUNKS
    z = lax.axis_index("seq")
    me = lax.axis_index("dom")
    last = seq_size - 1

    barrier = pltpu.get_barrier_semaphore()

    @pl.when(z > 0)
    def _():
        pl.semaphore_signal(barrier, inc=1, device_id=(z - 1, me), device_id_type=MESH)

    @pl.when(z < last)
    def _():
        pl.semaphore_signal(barrier, inc=1, device_id=(z + 1, me), device_id_type=MESH)

    for o in range(1, dom_size):
        pl.semaphore_signal(
            barrier, inc=1, device_id=(z, lax.rem(me + o, dom_size)), device_id_type=MESH
        )

    step = BLK
    held = rows // BLK
    for r in range(0, rows, step):
        wide = nodes_ref[r : r + step, :].astype(jnp.float32)
        center = jnp.mean(wide, axis=-1, keepdims=True)
        moved = wide - center
        spread = jnp.mean(jnp.square(moved), axis=-1, keepdims=True)
        normed = (moved * lax.rsqrt(spread + 1e-05) * gain_ref[...]).astype(jnp.bfloat16)
        for c in range(CHUNKS):
            local[c][z * held + r // step] = normed[:, c * cw : (c + 1) * cw]

    @pl.when((z > 0) & (z < last))
    def _():
        pl.semaphore_wait(barrier, dom_size + 1)

    @pl.when((z == 0) | (z == last))
    def _():
        pl.semaphore_wait(barrier, dom_size)

    def along(c, d, t):
        source = z - (t - 1) if d == 0 else z + (t - 1)
        target = z + 1 if d == 0 else z - 1
        block = local[c].at[pl.ds(source * held, held)]
        return pltpu.make_async_remote_copy(
            src_ref=block,
            dst_ref=block,
            send_sem=zsend.at[d, t - 1, c],
            recv_sem=zrecv.at[d, t - 1, c],
            device_id=(target, me),
            device_id_type=MESH,
        )

    def arriving(c, d, t):
        source = z - t if d == 0 else z + t
        block = local[c].at[pl.ds(source * held, held)]
        return pltpu.make_async_remote_copy(
            src_ref=block,
            dst_ref=block,
            send_sem=zsend.at[d, t - 1, c],
            recv_sem=zrecv.at[d, t - 1, c],
            device_id=(z - 1 if d == 0 else z + 1, me),
            device_id_type=MESH,
        )

    def sends(d, t):
        return (z >= t - 1) & (z < last) if d == 0 else (z <= last - (t - 1)) & (z > 0)

    def gets(d, t):
        return z >= t if d == 0 else z <= last - t

    def begin(c):
        for d in range(2):

            @pl.when(sends(d, 1))
            def _():
                along(c, d, 1).start()

    def across(c, o):
        target = lax.rem(me + o, dom_size)
        return pltpu.make_async_remote_copy(
            src_ref=stage.at[c, o - 1],
            dst_ref=remote.at[c, pl.ds(me * CAP, CAP)],
            send_sem=dsend.at[c, o - 1],
            recv_sem=drecv.at[c, o - 1],
            device_id=(z, target),
            device_id_type=MESH,
        )

    begin(0)
    if CHUNKS > 1:
        begin(1)
    for c in range(CHUNKS):
        for k in range(CAP):
            remote[c, me * CAP + k] = jnp.zeros((BLK, cw), jnp.bfloat16)
    for c in range(CHUNKS):
        for t in range(1, seq_size):
            for d in range(2):

                @pl.when(gets(d, t))
                def _():
                    arriving(c, d, t).wait_recv()

                if t < last:

                    @pl.when(sends(d, t + 1))
                    def _():
                        along(c, d, t + 1).start()

        if c + 2 < CHUNKS:
            begin(c + 2)
        for o in range(1, dom_size):
            target = lax.rem(me + o, dom_size)
            for k in range(CAP):
                block = pick_ref[target * CAP + k]
                stage[c, o - 1, k] = local[c][block]
            across(c, o).start()
    for c in range(CHUNKS):
        for o in range(1, dom_size):
            source = lax.rem(me + dom_size - o, dom_size)
            pltpu.make_async_remote_copy(
                src_ref=stage.at[c, o - 1],
                dst_ref=remote.at[c, pl.ds(source * CAP, CAP)],
                send_sem=dsend.at[c, o - 1],
                recv_sem=drecv.at[c, o - 1],
                device_id=(z, source),
                device_id_type=MESH,
            ).wait_recv()
            across(c, o).wait_send()
        for t in range(1, seq_size):
            for d in range(2):

                @pl.when(sends(d, t))
                def _():
                    along(c, d, t).wait_send()


def gather_rows(seq_size, dom_size, picks, node_rows, norm_gain):
    rows, width = node_rows.shape
    cw = width // CHUNKS
    vmem = pl.BlockSpec(memory_space=pltpu.VMEM)
    out = [jax.ShapeDtypeStruct((rows * seq_size // BLK, BLK, cw), jnp.bfloat16)] * CHUNKS
    out.append(jax.ShapeDtypeStruct((CHUNKS, dom_size * CAP, BLK, cw), jnp.bfloat16))
    return pl.pallas_call(
        functools.partial(gather_kernel, seq_size, dom_size),
        out_shape=out,
        in_specs=[pl.BlockSpec(memory_space=pltpu.SMEM), vmem, vmem],
        out_specs=[vmem] * (CHUNKS + 1),
        scratch_shapes=[
            pltpu.VMEM((CHUNKS, dom_size - 1, CAP, BLK, cw), jnp.bfloat16),
            pltpu.SemaphoreType.DMA((2, seq_size - 1, CHUNKS)),
            pltpu.SemaphoreType.DMA((2, seq_size - 1, CHUNKS)),
            pltpu.SemaphoreType.DMA((CHUNKS, dom_size - 1)),
            pltpu.SemaphoreType.DMA((CHUNKS, dom_size - 1)),
        ],
        compiler_params=pltpu.CompilerParams(
            collective_id=0, has_side_effects=True, vmem_limit_bytes=56 * 2**20
        ),
        name="gather_rows",
    )(picks, node_rows, norm_gain)


def attend_kernel(table_ref, meta_ref, *refs):
    local = refs[:CHUNKS]
    remote, w_ref, wo_ref, gain_ref, out_ref, k_ref, vt_ref, s_ref, mapped_ref = refs[CHUNKS:]
    g = pl.program_id(0)
    rows = out_ref.shape[0]
    local_blocks = local[0].shape[0]
    remote_blocks = remote.shape[1]
    wk = w_ref[1]
    wvt = w_ref[2].T

    def keep(x, base):
        n = x.shape[0]
        k_ref[pl.ds(pl.multiple_of(base * BLK, BLK), n), :] = dot(x, wk).astype(jnp.bfloat16)
        vt = dot(wvt, x, ((1,), (1,))).astype(jnp.bfloat16)
        for i in range(n // BLK):
            vt_ref[base + i] = vt[:, i * BLK : (i + 1) * BLK]

    def project(refs, base, count):
        step = max(n for n in range(1, 9) if count % n == 0)

        @pl.loop(0, count // step)
        def _(i):
            at = pl.ds(i * step, step)
            x = jnp.concatenate([c[at].reshape(step * BLK, -1) for c in refs], axis=1)
            keep(x, base + i * step)

    project(local, 0, local_blocks)
    project([remote.at[c] for c in range(CHUNKS)], local_blocks, remote_blocks)

    mine = pl.ds(meta_ref[0], rows // BLK)
    queries = dot(jnp.concatenate([c[mine].reshape(rows, -1) for c in local], axis=1), w_ref[0])
    queries = queries.astype(jnp.bfloat16) * jnp.bfloat16(HD**-0.5)

    head_of = lax.broadcasted_iota(jnp.int32, (GW, BLK), 0) // HD
    def score(b):
        qt = queries[b * BLK : (b + 1) * BLK, :].astype(jnp.float32).T
        spread = jnp.concatenate(
            [jnp.where(head_of == h, qt, 0.0) for h in range(GH)], axis=1
        ).astype(jnp.bfloat16)
        peak = None
        for j in range(KMAX):
            entry = table_ref[b * KMAX + j]
            keys = k_ref[pl.ds(pl.multiple_of(entry * BLK, BLK), BLK), :]
            scores = dot(keys, spread)
            if j >= KMAX - 4:
                scores = jnp.where(j < meta_ref[1 + b], scores, -jnp.inf)
            s_ref[b % 2, j] = scores
            top = jnp.max(scores.reshape(BLK // 8, 8, GH * BLK), axis=0)
            peak = top if peak is None else jnp.maximum(peak, top)
        return jnp.max(peak, axis=0, keepdims=True)

    def blend(b, peak):
        total = jnp.zeros((8, GH * BLK), jnp.float32)
        mix = jnp.zeros((GW, GH * BLK), jnp.float32)
        for j in range(0, KMAX, 2):
            parts = [jnp.exp(s_ref[b % 2, j + i] - peak) for i in range(2)]
            total += jnp.sum((parts[0] + parts[1]).reshape(BLK // 8, 8, GH * BLK), axis=0)
            weights = jnp.concatenate([p.astype(jnp.bfloat16) for p in parts], axis=0)
            values = jnp.concatenate([vt_ref[table_ref[b * KMAX + j + i]] for i in range(2)], axis=1)
            mix += dot(values, weights)
        scale = 1.0 / jnp.sum(total, axis=0, keepdims=True)
        attended = jnp.concatenate(
            [
                mix[h * HD : (h + 1) * HD, h * BLK : (h + 1) * BLK] * scale[:, h * BLK : (h + 1) * BLK]
                for h in range(GH)
            ],
            axis=0,
        )
        term = dot(attended.T.astype(jnp.bfloat16), wo_ref[...])
        at = slice(b * BLK, (b + 1) * BLK)
        mapped_ref[at, :] = jnp.where(g == 0, 0.0, mapped_ref[at, :]) + term

    query_blocks = rows // BLK
    peak = score(0)
    for b in range(query_blocks):
        later = score(b + 1) if b + 1 < query_blocks else None
        blend(b, peak)
        peak = later

    @pl.when(g == pl.num_programs(0) - 1)
    def _():
        mapped = mapped_ref[...]
        spread = jnp.mean(jnp.square(mapped), axis=-1, keepdims=True)
        out_ref[...] = (mapped * lax.rsqrt(spread + 1e-05) * gain_ref[...]).astype(jnp.bfloat16)


def attend_rows(table, meta, local, remote, weights, output_proj, final_gain, rows):
    width = output_proj.shape[0]
    blocks = local[0].shape[0] + remote.shape[1]
    vmem = pl.BlockSpec(memory_space=pltpu.VMEM)
    return pl.pallas_call(
        attend_kernel,
        out_shape=jax.ShapeDtypeStruct((rows, width), jnp.bfloat16),
        grid_spec=pltpu.PrefetchScalarGridSpec(
            num_scalar_prefetch=2,
            grid=(width // GW,),
            in_specs=[vmem] * (CHUNKS + 1)
            + [
                pl.BlockSpec((3, width, GW), lambda g, *_: (0, 0, g)),
                pl.BlockSpec((GW, width), lambda g, *_: (g, 0)),
                vmem,
            ],
            out_specs=pl.BlockSpec((rows, width), lambda g, *_: (0, 0)),
            scratch_shapes=[
                pltpu.VMEM((blocks * BLK, GW), jnp.bfloat16),
                pltpu.VMEM((blocks, GW, BLK), jnp.bfloat16),
                pltpu.VMEM((2, KMAX, BLK, GH * BLK), jnp.float32),
                pltpu.VMEM((rows, width), jnp.float32),
            ],
        ),
        compiler_params=pltpu.CompilerParams(vmem_limit_bytes=60 * 2**20),
        name="attend_rows",
    )(table, meta, *local, remote, weights, output_proj, final_gain)


def plan_lists(block_list, block_count, blocks_here, query_blocks):
    dom_size = lax.axis_size("dom")
    me = lax.axis_index("dom")
    z = lax.axis_index("seq")
    live = jnp.arange(KMAX)[None, :] < block_count[:, None]
    listed = jnp.where(live, block_list, -1).reshape(dom_size, blocks_here * KMAX)
    mine = me * blocks_here + jnp.arange(blocks_here)
    asked = jnp.any(listed[:, :, None] == mine[None, None, :], axis=1)
    before = jnp.arange(blocks_here)[:, None] < jnp.arange(blocks_here)[None, :]
    rank = jnp.sum(asked[:, :, None] & before[None], axis=1, dtype=jnp.int32)
    hit = asked[:, None, :] & (rank[:, None, :] == jnp.arange(CAP)[None, :, None])
    picks = jnp.sum(jnp.where(hit, jnp.arange(blocks_here)[None, None, :], 0), axis=2)
    every = jnp.arange(dom_size * blocks_here)
    ours = lax.dynamic_slice_in_dim(listed, me, 1, 0).reshape(-1)
    wanted = jnp.any(ours[:, None] == every[None, :], axis=0)
    entries = lax.dynamic_slice_in_dim(ours, z * query_blocks * KMAX, query_blocks * KMAX)
    safe = jnp.where(entries >= 0, entries, me * blocks_here)
    source = safe // blocks_here
    lower = (every[None, :] < safe[:, None]) & (every[None, :] >= (source * blocks_here)[:, None])
    slot = jnp.sum(lower & wanted[None, :], axis=1, dtype=jnp.int32)
    table = jnp.where(source == me, safe - me * blocks_here, blocks_here + source * CAP + slot)
    counts = lax.dynamic_slice_in_dim(block_count, me * blocks_here + z * query_blocks, query_blocks)
    meta = jnp.concatenate([jnp.reshape(z * query_blocks, (1,)), counts])
    return picks.reshape(-1), table.astype(jnp.int32), meta.astype(jnp.int32)


AHEAD = 2
UNIT = 16
SPLIT = 64
FAR = 2**30


def fused_kernel(
    seq_size, dom_size, lists_ref, entries_ref, counts_ref, gain_ref, final_ref, nodes_hbm, w_hbm, wo_hbm,
    out_ref, nodes_ref, x_ref, snap_ref, stage_ref, w_ref, kv_ref, q_ref, s_ref, peak_ref, sum_ref, near_ref,
    att_ref, pick_ref, first_ref, table_ref, zsend, zrecv, dsend, drecv, wsem,
):
    rows, width = nodes_ref.shape
    held = rows // BLK
    local_blocks = held * seq_size
    far_blocks = dom_size * CAP
    units = BLK // UNIT
    groups = width // GW
    heads = GH * BLK
    z = lax.axis_index("seq")
    me = lax.axis_index("dom")
    last = seq_size - 1

    barrier = pltpu.get_barrier_semaphore()

    @pl.when(z > 0)
    def _():
        pl.semaphore_signal(barrier, inc=1, device_id=(z - 1, me), device_id_type=MESH)

    @pl.when(z < last)
    def _():
        pl.semaphore_signal(barrier, inc=1, device_id=(z + 1, me), device_id_type=MESH)

    for o in range(1, dom_size):
        pl.semaphore_signal(
            barrier, inc=1, device_id=(z, lax.rem(me + o, dom_size)), device_id_type=MESH
        )

    load_nodes = pltpu.make_async_copy(nodes_hbm, nodes_ref, wsem.at[4])
    load_nodes.start()
    loads = [pltpu.make_async_copy(w_hbm.at[i], w_ref.at[i], wsem.at[i]) for i in range(3)]
    load_out = pltpu.make_async_copy(wo_hbm, w_ref.at[0], wsem.at[3])
    for load in loads:
        load.start()

    def normalize(first, end):
        for r in range(held):
            wide = nodes_ref[r * BLK + first * UNIT : r * BLK + end * UNIT, :].astype(jnp.float32)
            center = jnp.mean(wide, axis=-1, keepdims=True)
            moved = wide - center
            spread = jnp.mean(jnp.square(moved), axis=-1, keepdims=True)
            normed = (moved * lax.rsqrt(spread + 1e-05) * gain_ref[...]).astype(jnp.bfloat16)
            for u in range(first, end):
                x_ref[u, z * held + r] = normed[(u - first) * UNIT : (u - first + 1) * UNIT, :]

    load_nodes.wait()
    normalize(0, AHEAD)

    @pl.when((z > 0) & (z < last))
    def _():
        pl.semaphore_wait(barrier, dom_size + 1)

    @pl.when((z == 0) | (z == last))
    def _():
        pl.semaphore_wait(barrier, dom_size)

    def hop(u, d, t, source, target):
        block = x_ref.at[u, pl.ds(source * held, held)]
        return pltpu.make_async_remote_copy(
            src_ref=block,
            dst_ref=block,
            send_sem=zsend.at[d, t - 1, u],
            recv_sem=zrecv.at[d, t - 1, u],
            device_id=(target, me),
            device_id_type=MESH,
        )

    def along(u, d, t):
        return hop(u, d, t, z - (t - 1) if d == 0 else z + (t - 1), z + 1 if d == 0 else z - 1)

    def arriving(u, d, t):
        return hop(u, d, t, z - t if d == 0 else z + t, z - 1 if d == 0 else z + 1)

    def sends(d, t):
        return (z >= t - 1) & (z < last) if d == 0 else (z <= last - (t - 1)) & (z > 0)

    def gets(d, t):
        return z >= t if d == 0 else z <= last - t

    def begin(u, inner):
        for d in range(2):
            edge = 0 if d == 0 else last

            @pl.when(sends(d, 1) & ((z != edge) if inner else (z == edge)))
            def _():
                along(u, d, 1).start()

    def picked(u, o, source, partner):
        return pltpu.make_async_remote_copy(
            src_ref=stage_ref.at[u, o - 1],
            dst_ref=x_ref.at[u, pl.ds(local_blocks + source * CAP, CAP)],
            send_sem=dsend.at[u, o - 1],
            recv_sem=drecv.at[u, o - 1],
            device_id=(z, partner),
            device_id_type=MESH,
        )

    def across(u, o):
        return picked(u, o, me, lax.rem(me + o, dom_size))

    def take(u):
        for o in range(1, dom_size):
            source = lax.rem(me + dom_size - o, dom_size)
            picked(u, o, source, source).wait_recv()

    for u in range(AHEAD):
        begin(u, False)
        begin(u, True)
    normalize(AHEAD, units)
    for u in range(AHEAD, units):
        begin(u, False)

    lists = lists_ref[...]
    lane = lax.broadcasted_iota(jnp.int32, lists.shape, 1)
    mine = (lists >= me * local_blocks) & (lists < (me + 1) * local_blocks)
    for o in range(1, dom_size):
        target = lax.rem(me + o, dom_size)
        theirs = (lane >= target * local_blocks) & (lane < (target + 1) * local_blocks)
        low = jnp.min(jnp.where(mine & theirs, lists, FAR))
        high = jnp.max(jnp.where(mine & theirs, lists, -1))
        pick_ref[(o - 1) * CAP] = jnp.where(low < FAR, low - me * local_blocks, 0)
        pick_ref[(o - 1) * CAP + 1] = jnp.where(high >= 0, high - me * local_blocks, 0)
    ours = (lane >= me * local_blocks) & (lane < (me + 1) * local_blocks)
    for s in range(dom_size):
        inside = (lists >= s * local_blocks) & (lists < (s + 1) * local_blocks)
        first_ref[s] = jnp.min(jnp.where(ours & inside, lists, FAR))
    at = me * local_blocks + z * held
    for b in range(held):
        for j in range(KMAX):
            entry = entries_ref[j, at + b]
            slot = z * held + b
            if j < NEAR:
                inside = (entry >= me * local_blocks) & (entry < (me + 1) * local_blocks)
                table_ref[b * KMAX + j] = jnp.where(inside, entry - me * local_blocks, slot)
            else:
                for s in range(dom_size):
                    place = local_blocks + s * CAP + jnp.where(entry == first_ref[s], 0, 1)
                    inside = (entry >= s * local_blocks) & (entry < (s + 1) * local_blocks)
                    slot = jnp.where(inside, place, slot)
                table_ref[b * KMAX + j] = slot

    for u in range(units):
        for k in range(CAP):
            x_ref[u, local_blocks + me * CAP + k] = jnp.zeros((UNIT, width), jnp.bfloat16)

    def project(kv, first, count, u, n):
        blocks = slice(first, first + count)
        x = x_ref[pl.ds(u, n), blocks].reshape(n * count * UNIT, width)
        for g in range(groups):
            cols = slice(g * GW, (g + 1) * GW)
            made = dot(x, w_ref[1 + kv, :, cols]).astype(jnp.bfloat16).reshape(n, count, UNIT, GW)
            for i in range(n):
                at_rows = pl.ds(pl.multiple_of((u + i) * UNIT, UNIT), UNIT)
                kv_ref[kv, blocks, at_rows, cols] = made[i]

    def project_queries():
        for load in loads:
            load.wait()
        x = x_ref[:, pl.ds(z * held, held)].reshape(rows, width)
        for g in range(groups):
            cols = slice(g * GW, (g + 1) * GW)
            made = dot(x, w_ref[0, :, cols]).astype(jnp.bfloat16) * jnp.bfloat16(HD**-0.5)
            q_ref[:, :, :, cols] = made.reshape(units, held, UNIT, GW)
        load_out.start()

    head_of = lax.broadcasted_iota(jnp.int32, (BLK, GW), 1) // HD

    def attend(b, start, end):
        span = end - start
        tiles = KMAX * span // BLK
        each = BLK // span
        nth = lax.broadcasted_iota(jnp.int32, (1, BLK), 1) // span

        def gathered(kv, g, tile, n):
            entries = range(tile * each, (tile + n) * each)
            return jnp.concatenate(
                [kv_ref[kv, table_ref[b * KMAX + j], start:end, g * GW : (g + 1) * GW] for j in entries],
                axis=0,
            )

        def spans():
            return [(i, min(2, tiles - i)) for i in range(0, tiles, 2)]

        def score(g):
            q = q_ref[:, b, :, g * GW : (g + 1) * GW].reshape(BLK, GW)
            wide = jnp.concatenate([jnp.where(head_of == h, q, jnp.bfloat16(0)) for h in range(GH)], axis=0)
            peak = None
            for tile, n in spans():
                both = dot(wide, gathered(0, g, tile, n), ((1,), (1,)))
                for i in range(n):
                    scores = both[:, i * BLK : (i + 1) * BLK]
                    if (tile + i + 1) * each > KMAX - 4:
                        live = nth + (tile + i) * each < counts_ref[at + b]
                        scores = jnp.where(live, scores, -jnp.inf)
                    s_ref[(g % 2) * MOST + tile + i] = scores
                    peak = scores if peak is None else jnp.maximum(peak, scores)
            peak = jnp.broadcast_to(jnp.max(peak, axis=1, keepdims=True), (heads, BLK))
            return peak if start == 0 else jnp.maximum(peak, peak_ref[b * groups + g])

        def blend(g, peak):
            total = jnp.zeros((heads, BLK), jnp.float32)
            mix = jnp.zeros((heads, GW), jnp.float32)
            for tile, n in spans():
                parts = [jnp.exp(s_ref[(g % 2) * MOST + tile + i] - peak) for i in range(n)]
                for part in parts:
                    total += part
                weights = jnp.concatenate([part.astype(jnp.bfloat16) for part in parts], axis=1)
                mix += dot(weights, gathered(1, g, tile, n))
            return jnp.broadcast_to(jnp.sum(total, axis=1, keepdims=True), (heads, BLK)), mix

        def own_heads(part_of):
            kept = part_of(GH - 1)
            for h in range(GH - 1):
                kept = jnp.where(head_of == h, part_of(h), kept)
            return kept

        def rows_of(x, h):
            return x[h * BLK : (h + 1) * BLK]

        def over(x, h):
            return jnp.concatenate([rows_of(x, h)] * (GW // BLK), axis=1)

        peak = score(0)
        for g in range(groups):
            n = b * groups + g
            later = score(g + 1) if g + 1 < groups else None
            total, mix = blend(g, peak)
            kept = own_heads(lambda h: rows_of(mix, h))
            if start > 0:
                fade = jnp.exp(peak_ref[n] - peak)
                total = total + sum_ref[n] * fade
                kept = kept + near_ref[n] * own_heads(lambda h: over(fade, h))
            if end == BLK:
                kept = kept / own_heads(lambda h: over(total, h))
            if end == BLK:
                at_rows = pl.ds(pl.multiple_of(b * BLK, BLK), BLK)
                att_ref[at_rows, g * GW : (g + 1) * GW] = kept.astype(jnp.bfloat16)
            else:
                peak_ref[n] = peak
                sum_ref[n] = total
                near_ref[n] = kept
            peak = later

    @pl.loop(0, units)
    def _(u):
        odd = lax.rem(u, 2)
        for t in range(1, seq_size):
            for d in range(2):

                @pl.when(gets(d, t))
                def _():
                    arriving(u, d, t).wait_recv()

                if t < last:

                    @pl.when(sends(d, t + 1))
                    def _():
                        along(u, d, t + 1).start()

            if t == last:

                @pl.when(u + AHEAD < units)
                def _():
                    begin(u + AHEAD, True)

                snap_ref[...] = x_ref[u, 0:local_blocks]
                for o in range(1, dom_size):
                    for k in range(CAP):
                        stage_ref[u, o - 1, k] = snap_ref[pick_ref[(o - 1) * CAP + k]]
                    across(u, o).start()

                @pl.when(u == 0)
                def _():
                    project_queries()

            for kv in range(2):
                if t == min(kv + 1, last):

                    @pl.when((u >= 2) & (odd == 0))
                    def _():
                        project(kv, 0, local_blocks, u - 2, 2)

                    @pl.when((u >= 3) & (odd == 1))
                    def _():
                        if kv == 0:
                            take(u - 3)
                            take(u - 2)
                        project(kv, local_blocks, far_blocks, u - 3, 2)

            if t == last:

                @pl.when(u >= units - 2)
                def _():
                    late = u - (units - 2)
                    most = held - held // 2

                    @pl.loop(late * most, most + late * (held - most))
                    def _(b):
                        attend(b, 0, SPLIT)

    for kv in range(2):
        project(kv, 0, local_blocks, units - 2, 2)

    @pl.loop(units - 2, units)
    def _(u):
        take(u)
        for kv in range(2):
            project(kv, local_blocks, far_blocks, u, 1)

    @pl.loop(0, held)
    def _(b):
        attend(b, SPLIT, BLK)

    load_out.wait()
    part = GW // BLK
    squares = jnp.zeros((rows, BLK), jnp.float32)
    for g in range(groups):
        mapped = dot(att_ref[...], w_ref[0, :, g * GW : (g + 1) * GW])
        for i in range(part):
            piece_of = mapped[:, i * BLK : (i + 1) * BLK]
            s_ref[g * part + i, 0:rows, :] = piece_of
            squares += jnp.square(piece_of)
    norm = lax.rsqrt(jnp.sum(squares, axis=1, keepdims=True) * (1.0 / width) + 1e-05)
    for i in range(groups * part):
        cols = slice(i * BLK, (i + 1) * BLK)
        out_ref[:, cols] = (s_ref[i, 0:rows, :] * norm * final_ref[:, cols]).astype(jnp.bfloat16)

    @pl.loop(0, units)
    def _(u):
        for o in range(1, dom_size):
            across(u, o).wait_send()
        for t in range(1, seq_size):
            for d in range(2):

                @pl.when(sends(d, t))
                def _():
                    along(u, d, t).wait_send()


MOST = KMAX * max(SPLIT, BLK - SPLIT) // BLK


def fused_scratch(seq_size, dom_size, rows, width):
    units = BLK // UNIT
    held = rows // BLK
    local_blocks = held * seq_size
    blocks = local_blocks + dom_size * CAP
    steps = held * (width // GW)
    heads = GH * BLK
    f32, bf16, i32 = jnp.float32, jnp.bfloat16, jnp.int32
    arrays = [
        ((rows, width), bf16),
        ((units, blocks, UNIT, width), bf16),
        ((local_blocks, UNIT, width), bf16),
        ((units, dom_size - 1, CAP, UNIT, width), bf16),
        ((3, width, width), bf16),
        ((2, blocks, BLK, width), bf16),
        ((units, held, UNIT, width), bf16),
        ((2 * MOST, heads, BLK), f32),
        ((steps, heads, BLK), f32),
        ((steps, heads, BLK), f32),
        ((steps, BLK, GW), f32),
        ((rows, width), bf16),
    ]
    size = sum(math.prod(shape) * jnp.dtype(kind).itemsize for shape, kind in arrays)
    scratch = [pltpu.VMEM(shape, kind) for shape, kind in arrays]
    scratch += [pltpu.SMEM((n,), i32) for n in (CAP * (dom_size - 1), dom_size, held * KMAX)]
    scratch += [
        pltpu.SemaphoreType.DMA((2, seq_size - 1, units)),
        pltpu.SemaphoreType.DMA((2, seq_size - 1, units)),
        pltpu.SemaphoreType.DMA((units, dom_size - 1)),
        pltpu.SemaphoreType.DMA((units, dom_size - 1)),
        pltpu.SemaphoreType.DMA((5,)),
    ]
    return scratch, width <= BLK * 2 * MOST and rows <= heads and size < 51 * 2**20


def fused_layer(seq_size, dom_size, scratch, node_rows, norm_gain, weights, output_proj, final_gain, lists, counts):
    vmem = pl.BlockSpec(memory_space=pltpu.VMEM)
    smem = pl.BlockSpec(memory_space=pltpu.SMEM)
    hbm = pl.BlockSpec(memory_space=pl.ANY)
    return pl.pallas_call(
        functools.partial(fused_kernel, seq_size, dom_size),
        out_shape=jax.ShapeDtypeStruct(node_rows.shape, jnp.bfloat16),
        in_specs=[vmem, smem, smem, vmem, vmem, hbm, hbm, hbm],
        out_specs=vmem,
        scratch_shapes=scratch,
        compiler_params=pltpu.CompilerParams(
            collective_id=1, has_side_effects=True, vmem_limit_bytes=60 * 2**20
        ),
        name="fused_layer",
    )(lists, lists, counts, norm_gain, final_gain, node_rows, weights, output_proj)


def on_device(nodes, norm_gain, input_proj, output_proj, final_gain, block_list, block_count):
    node_rows = nodes[0]
    rows = node_rows.shape[0]
    seq_size = lax.axis_size("seq")
    dom_size = lax.axis_size("dom")
    weights = jnp.transpose(input_proj, (1, 0, 2))
    scratch, fits = fused_scratch(seq_size, dom_size, rows, node_rows.shape[1])
    if fits:
        out = fused_layer(
            seq_size, dom_size, scratch, node_rows, norm_gain[None, :], weights, output_proj,
            final_gain[None, :], block_list.T, block_count,
        )
        return out[None]
    blocks_here = rows * seq_size // BLK
    picks, table, meta = plan_lists(block_list, block_count, blocks_here, rows // BLK)
    *local, remote = gather_rows(seq_size, dom_size, picks, node_rows, norm_gain[None, :])
    out = attend_rows(
        table, meta, local, remote, weights, output_proj, final_gain[None, :], rows,
    )
    return out[None]


def solution(mesh):
    placed = (P("dom", "seq", None), P(), P(), P(), P(), P(), P())
    return jax.shard_map(
        on_device, mesh=mesh, in_specs=placed, out_specs=P("dom", "seq", None), check_vma=False
    )
```

```python
import functools
import math

import jax
import jax.numpy as jnp
from jax import lax
from jax.experimental import pallas as pl
from jax.experimental.pallas import tpu as pltpu
from jax.sharding import PartitionSpec as P

HD = 64
BLK = 128
KMAX = 12
CAP = 2
NEAR = 4
GW = 256
GH = GW // HD
CHUNKS = 4
MESH = pl.DeviceIdType.MESH


def dot(a, b, dims=((1,), (0,))):
    return lax.dot_general(a, b, (dims, ((), ())), preferred_element_type=jnp.float32)


def gather_kernel(seq_size, dom_size, pick_ref, nodes_ref, gain_ref, *refs):
    local = refs[:CHUNKS]
    remote = refs[CHUNKS]
    stage, zsend, zrecv, dsend, drecv = refs[CHUNKS + 1 :]
    rows, width = nodes_ref.shape
    cw = width // CHUNKS
    z = lax.axis_index("seq")
    me = lax.axis_index("dom")
    last = seq_size - 1

    barrier = pltpu.get_barrier_semaphore()

    @pl.when(z > 0)
    def _():
        pl.semaphore_signal(barrier, inc=1, device_id=(z - 1, me), device_id_type=MESH)

    @pl.when(z < last)
    def _():
        pl.semaphore_signal(barrier, inc=1, device_id=(z + 1, me), device_id_type=MESH)

    for o in range(1, dom_size):
        pl.semaphore_signal(
            barrier, inc=1, device_id=(z, lax.rem(me + o, dom_size)), device_id_type=MESH
        )

    step = BLK
    held = rows // BLK
    for r in range(0, rows, step):
        wide = nodes_ref[r : r + step, :].astype(jnp.float32)
        center = jnp.mean(wide, axis=-1, keepdims=True)
        moved = wide - center
        spread = jnp.mean(jnp.square(moved), axis=-1, keepdims=True)
        normed = (moved * lax.rsqrt(spread + 1e-05) * gain_ref[...]).astype(jnp.bfloat16)
        for c in range(CHUNKS):
            local[c][z * held + r // step] = normed[:, c * cw : (c + 1) * cw]

    @pl.when((z > 0) & (z < last))
    def _():
        pl.semaphore_wait(barrier, dom_size + 1)

    @pl.when((z == 0) | (z == last))
    def _():
        pl.semaphore_wait(barrier, dom_size)

    def along(c, d, t):
        source = z - (t - 1) if d == 0 else z + (t - 1)
        target = z + 1 if d == 0 else z - 1
        block = local[c].at[pl.ds(source * held, held)]
        return pltpu.make_async_remote_copy(
            src_ref=block,
            dst_ref=block,
            send_sem=zsend.at[d, t - 1, c],
            recv_sem=zrecv.at[d, t - 1, c],
            device_id=(target, me),
            device_id_type=MESH,
        )

    def arriving(c, d, t):
        source = z - t if d == 0 else z + t
        block = local[c].at[pl.ds(source * held, held)]
        return pltpu.make_async_remote_copy(
            src_ref=block,
            dst_ref=block,
            send_sem=zsend.at[d, t - 1, c],
            recv_sem=zrecv.at[d, t - 1, c],
            device_id=(z - 1 if d == 0 else z + 1, me),
            device_id_type=MESH,
        )

    def sends(d, t):
        return (z >= t - 1) & (z < last) if d == 0 else (z <= last - (t - 1)) & (z > 0)

    def gets(d, t):
        return z >= t if d == 0 else z <= last - t

    def begin(c):
        for d in range(2):

            @pl.when(sends(d, 1))
            def _():
                along(c, d, 1).start()

    def across(c, o):
        target = lax.rem(me + o, dom_size)
        return pltpu.make_async_remote_copy(
            src_ref=stage.at[c, o - 1],
            dst_ref=remote.at[c, pl.ds(me * CAP, CAP)],
            send_sem=dsend.at[c, o - 1],
            recv_sem=drecv.at[c, o - 1],
            device_id=(z, target),
            device_id_type=MESH,
        )

    begin(0)
    if CHUNKS > 1:
        begin(1)
    for c in range(CHUNKS):
        for k in range(CAP):
            remote[c, me * CAP + k] = jnp.zeros((BLK, cw), jnp.bfloat16)
    for c in range(CHUNKS):
        for t in range(1, seq_size):
            for d in range(2):

                @pl.when(gets(d, t))
                def _():
                    arriving(c, d, t).wait_recv()

                if t < last:

                    @pl.when(sends(d, t + 1))
                    def _():
                        along(c, d, t + 1).start()

        if c + 2 < CHUNKS:
            begin(c + 2)
        for o in range(1, dom_size):
            target = lax.rem(me + o, dom_size)
            for k in range(CAP):
                block = pick_ref[target * CAP + k]
                stage[c, o - 1, k] = local[c][block]
            across(c, o).start()
    for c in range(CHUNKS):
        for o in range(1, dom_size):
            source = lax.rem(me + dom_size - o, dom_size)
            pltpu.make_async_remote_copy(
                src_ref=stage.at[c, o - 1],
                dst_ref=remote.at[c, pl.ds(source * CAP, CAP)],
                send_sem=dsend.at[c, o - 1],
                recv_sem=drecv.at[c, o - 1],
                device_id=(z, source),
                device_id_type=MESH,
            ).wait_recv()
            across(c, o).wait_send()
        for t in range(1, seq_size):
            for d in range(2):

                @pl.when(sends(d, t))
                def _():
                    along(c, d, t).wait_send()


def gather_rows(seq_size, dom_size, picks, node_rows, norm_gain):
    rows, width = node_rows.shape
    cw = width // CHUNKS
    vmem = pl.BlockSpec(memory_space=pltpu.VMEM)
    out = [jax.ShapeDtypeStruct((rows * seq_size // BLK, BLK, cw), jnp.bfloat16)] * CHUNKS
    out.append(jax.ShapeDtypeStruct((CHUNKS, dom_size * CAP, BLK, cw), jnp.bfloat16))
    return pl.pallas_call(
        functools.partial(gather_kernel, seq_size, dom_size),
        out_shape=out,
        in_specs=[pl.BlockSpec(memory_space=pltpu.SMEM), vmem, vmem],
        out_specs=[vmem] * (CHUNKS + 1),
        scratch_shapes=[
            pltpu.VMEM((CHUNKS, dom_size - 1, CAP, BLK, cw), jnp.bfloat16),
            pltpu.SemaphoreType.DMA((2, seq_size - 1, CHUNKS)),
            pltpu.SemaphoreType.DMA((2, seq_size - 1, CHUNKS)),
            pltpu.SemaphoreType.DMA((CHUNKS, dom_size - 1)),
            pltpu.SemaphoreType.DMA((CHUNKS, dom_size - 1)),
        ],
        compiler_params=pltpu.CompilerParams(
            collective_id=0, has_side_effects=True, vmem_limit_bytes=56 * 2**20
        ),
        name="gather_rows",
    )(picks, node_rows, norm_gain)


def attend_kernel(table_ref, meta_ref, *refs):
    local = refs[:CHUNKS]
    remote, w_ref, wo_ref, gain_ref, out_ref, k_ref, vt_ref, s_ref, mapped_ref = refs[CHUNKS:]
    g = pl.program_id(0)
    rows = out_ref.shape[0]
    local_blocks = local[0].shape[0]
    remote_blocks = remote.shape[1]
    wk = w_ref[1]
    wvt = w_ref[2].T

    def keep(x, base):
        n = x.shape[0]
        k_ref[pl.ds(pl.multiple_of(base * BLK, BLK), n), :] = dot(x, wk).astype(jnp.bfloat16)
        vt = dot(wvt, x, ((1,), (1,))).astype(jnp.bfloat16)
        for i in range(n // BLK):
            vt_ref[base + i] = vt[:, i * BLK : (i + 1) * BLK]

    def project(refs, base, count):
        step = max(n for n in range(1, 9) if count % n == 0)

        @pl.loop(0, count // step)
        def _(i):
            at = pl.ds(i * step, step)
            x = jnp.concatenate([c[at].reshape(step * BLK, -1) for c in refs], axis=1)
            keep(x, base + i * step)

    project(local, 0, local_blocks)
    project([remote.at[c] for c in range(CHUNKS)], local_blocks, remote_blocks)

    mine = pl.ds(meta_ref[0], rows // BLK)
    queries = dot(jnp.concatenate([c[mine].reshape(rows, -1) for c in local], axis=1), w_ref[0])
    queries = queries.astype(jnp.bfloat16) * jnp.bfloat16(HD**-0.5)

    head_of = lax.broadcasted_iota(jnp.int32, (GW, BLK), 0) // HD
    def score(b):
        qt = queries[b * BLK : (b + 1) * BLK, :].astype(jnp.float32).T
        spread = jnp.concatenate(
            [jnp.where(head_of == h, qt, 0.0) for h in range(GH)], axis=1
        ).astype(jnp.bfloat16)
        peak = None
        for j in range(KMAX):
            entry = table_ref[b * KMAX + j]
            keys = k_ref[pl.ds(pl.multiple_of(entry * BLK, BLK), BLK), :]
            scores = dot(keys, spread)
            if j >= KMAX - 4:
                scores = jnp.where(j < meta_ref[1 + b], scores, -jnp.inf)
            s_ref[b % 2, j] = scores
            top = jnp.max(scores.reshape(BLK // 8, 8, GH * BLK), axis=0)
            peak = top if peak is None else jnp.maximum(peak, top)
        return jnp.max(peak, axis=0, keepdims=True)

    def blend(b, peak):
        total = jnp.zeros((8, GH * BLK), jnp.float32)
        mix = jnp.zeros((GW, GH * BLK), jnp.float32)
        for j in range(0, KMAX, 2):
            parts = [jnp.exp(s_ref[b % 2, j + i] - peak) for i in range(2)]
            total += jnp.sum((parts[0] + parts[1]).reshape(BLK // 8, 8, GH * BLK), axis=0)
            weights = jnp.concatenate([p.astype(jnp.bfloat16) for p in parts], axis=0)
            values = jnp.concatenate([vt_ref[table_ref[b * KMAX + j + i]] for i in range(2)], axis=1)
            mix += dot(values, weights)
        scale = 1.0 / jnp.sum(total, axis=0, keepdims=True)
        attended = jnp.concatenate(
            [
                mix[h * HD : (h + 1) * HD, h * BLK : (h + 1) * BLK] * scale[:, h * BLK : (h + 1) * BLK]
                for h in range(GH)
            ],
            axis=0,
        )
        term = dot(attended.T.astype(jnp.bfloat16), wo_ref[...])
        at = slice(b * BLK, (b + 1) * BLK)
        mapped_ref[at, :] = jnp.where(g == 0, 0.0, mapped_ref[at, :]) + term

    query_blocks = rows // BLK
    peak = score(0)
    for b in range(query_blocks):
        later = score(b + 1) if b + 1 < query_blocks else None
        blend(b, peak)
        peak = later

    @pl.when(g == pl.num_programs(0) - 1)
    def _():
        mapped = mapped_ref[...]
        spread = jnp.mean(jnp.square(mapped), axis=-1, keepdims=True)
        out_ref[...] = (mapped * lax.rsqrt(spread + 1e-05) * gain_ref[...]).astype(jnp.bfloat16)


def attend_rows(table, meta, local, remote, weights, output_proj, final_gain, rows):
    width = output_proj.shape[0]
    blocks = local[0].shape[0] + remote.shape[1]
    vmem = pl.BlockSpec(memory_space=pltpu.VMEM)
    return pl.pallas_call(
        attend_kernel,
        out_shape=jax.ShapeDtypeStruct((rows, width), jnp.bfloat16),
        grid_spec=pltpu.PrefetchScalarGridSpec(
            num_scalar_prefetch=2,
            grid=(width // GW,),
            in_specs=[vmem] * (CHUNKS + 1)
            + [
                pl.BlockSpec((3, width, GW), lambda g, *_: (0, 0, g)),
                pl.BlockSpec((GW, width), lambda g, *_: (g, 0)),
                vmem,
            ],
            out_specs=pl.BlockSpec((rows, width), lambda g, *_: (0, 0)),
            scratch_shapes=[
                pltpu.VMEM((blocks * BLK, GW), jnp.bfloat16),
                pltpu.VMEM((blocks, GW, BLK), jnp.bfloat16),
                pltpu.VMEM((2, KMAX, BLK, GH * BLK), jnp.float32),
                pltpu.VMEM((rows, width), jnp.float32),
            ],
        ),
        compiler_params=pltpu.CompilerParams(vmem_limit_bytes=60 * 2**20),
        name="attend_rows",
    )(table, meta, *local, remote, weights, output_proj, final_gain)


def plan_lists(block_list, block_count, blocks_here, query_blocks):
    dom_size = lax.axis_size("dom")
    me = lax.axis_index("dom")
    z = lax.axis_index("seq")
    live = jnp.arange(KMAX)[None, :] < block_count[:, None]
    listed = jnp.where(live, block_list, -1).reshape(dom_size, blocks_here * KMAX)
    mine = me * blocks_here + jnp.arange(blocks_here)
    asked = jnp.any(listed[:, :, None] == mine[None, None, :], axis=1)
    before = jnp.arange(blocks_here)[:, None] < jnp.arange(blocks_here)[None, :]
    rank = jnp.sum(asked[:, :, None] & before[None], axis=1, dtype=jnp.int32)
    hit = asked[:, None, :] & (rank[:, None, :] == jnp.arange(CAP)[None, :, None])
    picks = jnp.sum(jnp.where(hit, jnp.arange(blocks_here)[None, None, :], 0), axis=2)
    every = jnp.arange(dom_size * blocks_here)
    ours = lax.dynamic_slice_in_dim(listed, me, 1, 0).reshape(-1)
    wanted = jnp.any(ours[:, None] == every[None, :], axis=0)
    entries = lax.dynamic_slice_in_dim(ours, z * query_blocks * KMAX, query_blocks * KMAX)
    safe = jnp.where(entries >= 0, entries, me * blocks_here)
    source = safe // blocks_here
    lower = (every[None, :] < safe[:, None]) & (every[None, :] >= (source * blocks_here)[:, None])
    slot = jnp.sum(lower & wanted[None, :], axis=1, dtype=jnp.int32)
    table = jnp.where(source == me, safe - me * blocks_here, blocks_here + source * CAP + slot)
    counts = lax.dynamic_slice_in_dim(block_count, me * blocks_here + z * query_blocks, query_blocks)
    meta = jnp.concatenate([jnp.reshape(z * query_blocks, (1,)), counts])
    return picks.reshape(-1), table.astype(jnp.int32), meta.astype(jnp.int32)


AHEAD = 2
UNIT = 16
SPLIT = 64
FAR = 2**30


def fused_kernel(
    seq_size, dom_size, lists_ref, entries_ref, counts_ref, gain_ref, final_ref, nodes_hbm, w_hbm, wo_hbm,
    out_ref, nodes_ref, x_ref, snap_ref, stage_ref, w_ref, kv_ref, q_ref, s_ref, peak_ref, sum_ref, near_ref,
    att_ref, pick_ref, first_ref, table_ref, zsend, zrecv, dsend, drecv, wsem,
):
    rows, width = nodes_ref.shape
    held = rows // BLK
    local_blocks = held * seq_size
    far_blocks = dom_size * CAP
    units = BLK // UNIT
    groups = width // GW
    heads = GH * BLK
    z = lax.axis_index("seq")
    me = lax.axis_index("dom")
    last = seq_size - 1

    barrier = pltpu.get_barrier_semaphore()

    @pl.when(z > 0)
    def _():
        pl.semaphore_signal(barrier, inc=1, device_id=(z - 1, me), device_id_type=MESH)

    @pl.when(z < last)
    def _():
        pl.semaphore_signal(barrier, inc=1, device_id=(z + 1, me), device_id_type=MESH)

    for o in range(1, dom_size):
        pl.semaphore_signal(
            barrier, inc=1, device_id=(z, lax.rem(me + o, dom_size)), device_id_type=MESH
        )

    load_nodes = pltpu.make_async_copy(nodes_hbm, nodes_ref, wsem.at[4])
    load_nodes.start()
    loads = [pltpu.make_async_copy(w_hbm.at[i], w_ref.at[i], wsem.at[i]) for i in range(3)]
    load_out = pltpu.make_async_copy(wo_hbm, w_ref.at[0], wsem.at[3])
    for load in loads:
        load.start()

    def normalize(first, end):
        for r in range(held):
            wide = nodes_ref[r * BLK + first * UNIT : r * BLK + end * UNIT, :].astype(jnp.float32)
            center = jnp.mean(wide, axis=-1, keepdims=True)
            moved = wide - center
            spread = jnp.mean(jnp.square(moved), axis=-1, keepdims=True)
            normed = (moved * lax.rsqrt(spread + 1e-05) * gain_ref[...]).astype(jnp.bfloat16)
            for u in range(first, end):
                x_ref[u, z * held + r] = normed[(u - first) * UNIT : (u - first + 1) * UNIT, :]

    load_nodes.wait()
    normalize(0, AHEAD)

    @pl.when((z > 0) & (z < last))
    def _():
        pl.semaphore_wait(barrier, dom_size + 1)

    @pl.when((z == 0) | (z == last))
    def _():
        pl.semaphore_wait(barrier, dom_size)

    def hop(u, d, t, source, target):
        block = x_ref.at[u, pl.ds(source * held, held)]
        return pltpu.make_async_remote_copy(
            src_ref=block,
            dst_ref=block,
            send_sem=zsend.at[d, t - 1, u],
            recv_sem=zrecv.at[d, t - 1, u],
            device_id=(target, me),
            device_id_type=MESH,
        )

    def along(u, d, t):
        return hop(u, d, t, z - (t - 1) if d == 0 else z + (t - 1), z + 1 if d == 0 else z - 1)

    def arriving(u, d, t):
        return hop(u, d, t, z - t if d == 0 else z + t, z - 1 if d == 0 else z + 1)

    def sends(d, t):
        return (z >= t - 1) & (z < last) if d == 0 else (z <= last - (t - 1)) & (z > 0)

    def gets(d, t):
        return z >= t if d == 0 else z <= last - t

    def begin(u, inner):
        for d in range(2):
            edge = 0 if d == 0 else last

            @pl.when(sends(d, 1) & ((z != edge) if inner else (z == edge)))
            def _():
                along(u, d, 1).start()

    def picked(u, o, source, partner):
        return pltpu.make_async_remote_copy(
            src_ref=stage_ref.at[u, o - 1],
            dst_ref=x_ref.at[u, pl.ds(local_blocks + source * CAP, CAP)],
            send_sem=dsend.at[u, o - 1],
            recv_sem=drecv.at[u, o - 1],
            device_id=(z, partner),
            device_id_type=MESH,
        )

    def across(u, o):
        return picked(u, o, me, lax.rem(me + o, dom_size))

    def take(u):
        for o in range(1, dom_size):
            source = lax.rem(me + dom_size - o, dom_size)
            picked(u, o, source, source).wait_recv()

    for u in range(AHEAD):
        begin(u, False)
        begin(u, True)
    normalize(AHEAD, units)
    for u in range(AHEAD, units):
        begin(u, False)

    lists = lists_ref[...]
    lane = lax.broadcasted_iota(jnp.int32, lists.shape, 1)
    mine = (lists >= me * local_blocks) & (lists < (me + 1) * local_blocks)
    for o in range(1, dom_size):
        target = lax.rem(me + o, dom_size)
        theirs = (lane >= target * local_blocks) & (lane < (target + 1) * local_blocks)
        low = jnp.min(jnp.where(mine & theirs, lists, FAR))
        high = jnp.max(jnp.where(mine & theirs, lists, -1))
        pick_ref[(o - 1) * CAP] = jnp.where(low < FAR, low - me * local_blocks, 0)
        pick_ref[(o - 1) * CAP + 1] = jnp.where(high >= 0, high - me * local_blocks, 0)
    ours = (lane >= me * local_blocks) & (lane < (me + 1) * local_blocks)
    for s in range(dom_size):
        inside = (lists >= s * local_blocks) & (lists < (s + 1) * local_blocks)
        first_ref[s] = jnp.min(jnp.where(ours & inside, lists, FAR))
    at = me * local_blocks + z * held
    for b in range(held):
        for j in range(KMAX):
            entry = entries_ref[j, at + b]
            slot = z * held + b
            if j < NEAR:
                inside = (entry >= me * local_blocks) & (entry < (me + 1) * local_blocks)
                table_ref[b * KMAX + j] = jnp.where(inside, entry - me * local_blocks, slot)
            else:
                for s in range(dom_size):
                    place = local_blocks + s * CAP + jnp.where(entry == first_ref[s], 0, 1)
                    inside = (entry >= s * local_blocks) & (entry < (s + 1) * local_blocks)
                    slot = jnp.where(inside, place, slot)
                table_ref[b * KMAX + j] = slot

    for u in range(units):
        for k in range(CAP):
            x_ref[u, local_blocks + me * CAP + k] = jnp.zeros((UNIT, width), jnp.bfloat16)

    def project(kv, first, count, u, n):
        blocks = slice(first, first + count)
        x = x_ref[pl.ds(u, n), blocks].reshape(n * count * UNIT, width)
        for g in range(groups):
            cols = slice(g * GW, (g + 1) * GW)
            made = dot(x, w_ref[1 + kv, :, cols]).astype(jnp.bfloat16).reshape(n, count, UNIT, GW)
            for i in range(n):
                at_rows = pl.ds(pl.multiple_of((u + i) * UNIT, UNIT), UNIT)
                kv_ref[kv, blocks, at_rows, cols] = made[i]

    def project_queries():
        for load in loads:
            load.wait()
        x = x_ref[:, pl.ds(z * held, held)].reshape(rows, width)
        for g in range(groups):
            cols = slice(g * GW, (g + 1) * GW)
            made = dot(x, w_ref[0, :, cols]).astype(jnp.bfloat16) * jnp.bfloat16(HD**-0.5)
            q_ref[:, :, :, cols] = made.reshape(units, held, UNIT, GW)
        load_out.start()

    head_of = lax.broadcasted_iota(jnp.int32, (BLK, GW), 1) // HD

    def attend(b, start, end):
        span = end - start
        tiles = KMAX * span // BLK
        each = BLK // span
        nth = lax.broadcasted_iota(jnp.int32, (1, BLK), 1) // span

        def gathered(kv, g, tile, n):
            entries = range(tile * each, (tile + n) * each)
            return jnp.concatenate(
                [kv_ref[kv, table_ref[b * KMAX + j], start:end, g * GW : (g + 1) * GW] for j in entries],
                axis=0,
            )

        def spans():
            return [(i, min(2, tiles - i)) for i in range(0, tiles, 2)]

        def score(g):
            q = q_ref[:, b, :, g * GW : (g + 1) * GW].reshape(BLK, GW)
            wide = jnp.concatenate([jnp.where(head_of == h, q, jnp.bfloat16(0)) for h in range(GH)], axis=0)
            peak = None
            for tile, n in spans():
                both = dot(wide, gathered(0, g, tile, n), ((1,), (1,)))
                for i in range(n):
                    scores = both[:, i * BLK : (i + 1) * BLK]
                    if (tile + i + 1) * each > KMAX - 4:
                        live = nth + (tile + i) * each < counts_ref[at + b]
                        scores = jnp.where(live, scores, -jnp.inf)
                    s_ref[(g % 2) * MOST + tile + i] = scores
                    peak = scores if peak is None else jnp.maximum(peak, scores)
            peak = jnp.broadcast_to(jnp.max(peak, axis=1, keepdims=True), (heads, BLK))
            return peak if start == 0 else jnp.maximum(peak, peak_ref[b * groups + g])

        def blend(g, peak):
            total = jnp.zeros((heads, BLK), jnp.float32)
            mix = jnp.zeros((heads, GW), jnp.float32)
            for tile, n in spans():
                parts = [jnp.exp(s_ref[(g % 2) * MOST + tile + i] - peak) for i in range(n)]
                for part in parts:
                    total += part
                weights = jnp.concatenate([part.astype(jnp.bfloat16) for part in parts], axis=1)
                mix += dot(weights, gathered(1, g, tile, n))
            return jnp.broadcast_to(jnp.sum(total, axis=1, keepdims=True), (heads, BLK)), mix

        def own_heads(part_of):
            kept = part_of(GH - 1)
            for h in range(GH - 1):
                kept = jnp.where(head_of == h, part_of(h), kept)
            return kept

        def rows_of(x, h):
            return x[h * BLK : (h + 1) * BLK]

        def over(x, h):
            return jnp.concatenate([rows_of(x, h)] * (GW // BLK), axis=1)

        peak = score(0)
        for g in range(groups):
            n = b * groups + g
            later = score(g + 1) if g + 1 < groups else None
            total, mix = blend(g, peak)
            kept = own_heads(lambda h: rows_of(mix, h))
            if start > 0:
                fade = jnp.exp(peak_ref[n] - peak)
                total = total + sum_ref[n] * fade
                kept = kept + near_ref[n] * own_heads(lambda h: over(fade, h))
            if end == BLK:
                kept = kept / own_heads(lambda h: over(total, h))
            if end == BLK:
                at_rows = pl.ds(pl.multiple_of(b * BLK, BLK), BLK)
                att_ref[at_rows, g * GW : (g + 1) * GW] = kept.astype(jnp.bfloat16)
            else:
                peak_ref[n] = peak
                sum_ref[n] = total
                near_ref[n] = kept
            peak = later

    @pl.loop(0, units)
    def _(u):
        odd = lax.rem(u, 2)
        for t in range(1, seq_size):
            for d in range(2):

                @pl.when(gets(d, t))
                def _():
                    arriving(u, d, t).wait_recv()

                if t < last:

                    @pl.when(sends(d, t + 1))
                    def _():
                        along(u, d, t + 1).start()

            if t == last:

                @pl.when(u + AHEAD < units)
                def _():
                    begin(u + AHEAD, True)

                snap_ref[...] = x_ref[u, 0:local_blocks]
                for o in sorted(range(1, dom_size), key=lambda o: abs(2 * o - dom_size)):
                    for k in range(CAP):
                        stage_ref[u, o - 1, k] = snap_ref[pick_ref[(o - 1) * CAP + k]]
                    across(u, o).start()

                @pl.when(u == 0)
                def _():
                    project_queries()

            for kv in range(2):
                if t == min(kv + 1, last):

                    @pl.when((u >= 2) & (odd == 0))
                    def _():
                        project(kv, 0, local_blocks, u - 2, 2)

                    @pl.when((u >= 3) & (odd == 1))
                    def _():
                        if kv == 0:
                            take(u - 3)
                            take(u - 2)
                        project(kv, local_blocks, far_blocks, u - 3, 2)

            if t == last:

                @pl.when(u >= units - 2)
                def _():
                    late = u - (units - 2)
                    most = held - held // 2

                    @pl.loop(late * most, most + late * (held - most))
                    def _(b):
                        attend(b, 0, SPLIT)

    for kv in range(2):
        project(kv, 0, local_blocks, units - 2, 2)

    @pl.loop(units - 2, units)
    def _(u):
        take(u)
        for kv in range(2):
            project(kv, local_blocks, far_blocks, u, 1)

    @pl.loop(0, held)
    def _(b):
        attend(b, SPLIT, BLK)

    load_out.wait()
    part = GW // BLK
    squares = jnp.zeros((rows, BLK), jnp.float32)
    for g in range(groups):
        mapped = dot(att_ref[...], w_ref[0, :, g * GW : (g + 1) * GW])
        for i in range(part):
            piece_of = mapped[:, i * BLK : (i + 1) * BLK]
            s_ref[g * part + i, 0:rows, :] = piece_of
            squares += jnp.square(piece_of)
    norm = lax.rsqrt(jnp.sum(squares, axis=1, keepdims=True) * (1.0 / width) + 1e-05)
    for i in range(groups * part):
        cols = slice(i * BLK, (i + 1) * BLK)
        out_ref[:, cols] = (s_ref[i, 0:rows, :] * norm * final_ref[:, cols]).astype(jnp.bfloat16)

    @pl.loop(0, units)
    def _(u):
        for o in range(1, dom_size):
            across(u, o).wait_send()
        for t in range(1, seq_size):
            for d in range(2):

                @pl.when(sends(d, t))
                def _():
                    along(u, d, t).wait_send()


MOST = KMAX * max(SPLIT, BLK - SPLIT) // BLK


def fused_scratch(seq_size, dom_size, rows, width):
    units = BLK // UNIT
    held = rows // BLK
    local_blocks = held * seq_size
    blocks = local_blocks + dom_size * CAP
    steps = held * (width // GW)
    heads = GH * BLK
    f32, bf16, i32 = jnp.float32, jnp.bfloat16, jnp.int32
    arrays = [
        ((rows, width), bf16),
        ((units, blocks, UNIT, width), bf16),
        ((local_blocks, UNIT, width), bf16),
        ((units, dom_size - 1, CAP, UNIT, width), bf16),
        ((3, width, width), bf16),
        ((2, blocks, BLK, width), bf16),
        ((units, held, UNIT, width), bf16),
        ((2 * MOST, heads, BLK), f32),
        ((steps, heads, BLK), f32),
        ((steps, heads, BLK), f32),
        ((steps, BLK, GW), f32),
        ((rows, width), bf16),
    ]
    size = sum(math.prod(shape) * jnp.dtype(kind).itemsize for shape, kind in arrays)
    scratch = [pltpu.VMEM(shape, kind) for shape, kind in arrays]
    scratch += [pltpu.SMEM((n,), i32) for n in (CAP * (dom_size - 1), dom_size, held * KMAX)]
    scratch += [
        pltpu.SemaphoreType.DMA((2, seq_size - 1, units)),
        pltpu.SemaphoreType.DMA((2, seq_size - 1, units)),
        pltpu.SemaphoreType.DMA((units, dom_size - 1)),
        pltpu.SemaphoreType.DMA((units, dom_size - 1)),
        pltpu.SemaphoreType.DMA((5,)),
    ]
    return scratch, width <= BLK * 2 * MOST and rows <= heads and size < 51 * 2**20


def fused_layer(seq_size, dom_size, scratch, node_rows, norm_gain, weights, output_proj, final_gain, lists, counts):
    vmem = pl.BlockSpec(memory_space=pltpu.VMEM)
    smem = pl.BlockSpec(memory_space=pltpu.SMEM)
    hbm = pl.BlockSpec(memory_space=pl.ANY)
    return pl.pallas_call(
        functools.partial(fused_kernel, seq_size, dom_size),
        out_shape=jax.ShapeDtypeStruct(node_rows.shape, jnp.bfloat16),
        in_specs=[vmem, smem, smem, vmem, vmem, hbm, hbm, hbm],
        out_specs=vmem,
        scratch_shapes=scratch,
        compiler_params=pltpu.CompilerParams(
            collective_id=1, has_side_effects=True, vmem_limit_bytes=60 * 2**20
        ),
        name="fused_layer",
    )(lists, lists, counts, norm_gain, final_gain, node_rows, weights, output_proj)


def on_device(nodes, norm_gain, input_proj, output_proj, final_gain, block_list, block_count):
    node_rows = nodes[0]
    rows = node_rows.shape[0]
    seq_size = lax.axis_size("seq")
    dom_size = lax.axis_size("dom")
    weights = jnp.transpose(input_proj, (1, 0, 2))
    scratch, fits = fused_scratch(seq_size, dom_size, rows, node_rows.shape[1])
    if fits:
        out = fused_layer(
            seq_size, dom_size, scratch, node_rows, norm_gain[None, :], weights, output_proj,
            final_gain[None, :], block_list.T, block_count,
        )
        return out[None]
    blocks_here = rows * seq_size // BLK
    picks, table, meta = plan_lists(block_list, block_count, blocks_here, rows // BLK)
    *local, remote = gather_rows(seq_size, dom_size, picks, node_rows, norm_gain[None, :])
    out = attend_rows(
        table, meta, local, remote, weights, output_proj, final_gain[None, :], rows,
    )
    return out[None]


def solution(mesh):
    placed = (P("dom", "seq", None), P(), P(), P(), P(), P(), P())
    return jax.shard_map(
        on_device, mesh=mesh, in_specs=placed, out_specs=P("dom", "seq", None), check_vma=False
    )
```
